256 devices in a mesh: seq: 64 (over z, y, x_hi), head: 4 (over x_lo, core).
Axes of the slice: x: 4 (x_hi: 2, x_lo: 2; x = x_hi * 2 + x_lo), y: 4, z: 8, core: 2. Of those that a mesh axis runs over, the one named last changes fastest.
Arguments:
- inputs: bfloat16 [5376, 8192], P(None, 'seq'), may hold values from -16 to 16
- queries: bfloat16 [8192, 4096], P('seq', 'head'), may hold values from -2000 to 2000
- keys: bfloat16 [8192, 2048], P('seq', 'head'), may hold values from -6 to 6
- values: bfloat16 [8192, 2048], P('seq', 'head'), may hold values from -6 to 6
- grad_out: bfloat16 [8192, 4096], P('seq', 'head'), may hold values from -6 to 6
- doc_ids: int32 [8192], replicated, may hold values from 0 to 15, never falling along the last dimension, each value on 1 to 1024 neighbouring positions
Outputs:
- grad_queries: bfloat16 [8192, 4096], P('seq', 'head')
- grad_keys: bfloat16 [8192, 2048], P('seq', 'head')
- grad_values: bfloat16 [8192, 2048], P('seq', 'head')
- grad_key_weight: float32 [5376, 2048], P('seq', 'head')
- grad_value_weight: float32 [5376, 2048], P('seq', 'head')
The draws below stay inside these ranges and needn't reach their ends.
Inputs may be any that keep to these rules, and one draw needn't show every extreme that they name: `doc_ids`: never falling along the sequence; each document holds at most (1024) tokens.
All inputs are finite; a program needn't handle non-finite values.
Results may differ from the reference program's by a relative error of at most 0.0053.
Values may be sent and summed in bfloat16 or wider, within the bound.
A program may use at most 128 MiB of HBM per device.

```python
import math
import jax
import jax.numpy as jnp
import numpy as np
from jax import lax

D = 5376
Q_HEADS = 32
KV_HEADS = 16
HEAD_DIM = 128
WINDOW = 1024
TOK_DEV = 128
SEQ = 8192
N_SEQ = 64


def shared_rows(key):
    base = jax.random.normal(jax.random.fold_in(key, 11), (SEQ, KV_HEADS, HEAD_DIM), jnp.float32)
    base = jnp.clip(base, -6.0, 6.0)
    return base


def draw_keys(key, part):
    base = shared_rows(key)
    return base.reshape(SEQ, KV_HEADS * HEAD_DIM).astype(jnp.bfloat16)


def draw_queries(key, part):
    key = jax.random.fold_in(key, 2)
    drawn = jax.random.normal(key, (SEQ, Q_HEADS, HEAD_DIM), jnp.float32)
    drawn = jnp.clip(drawn, -6.0, 6.0)
    return drawn.reshape(SEQ, Q_HEADS * HEAD_DIM).astype(jnp.bfloat16)


def raised(values, rng, source, target, blocks, factor):
    owner, partner = [(jnp.arange(values.shape[dim]) // (values.shape[dim] // blocks)).reshape([-1 if axis == dim else 1 for axis in range(values.ndim)]) for dim in (source, target)]
    chosen = jax.random.permutation(rng, blocks)[partner]
    strong = (owner == chosen) | (owner == (partner + blocks // 2) % blocks)
    return jnp.where(strong, factor * values, values)


def block_scale(own_key, dims, pieces, least, top_value):
    def one(dim, blocks):
        steps = jax.random.uniform(jax.random.fold_in(jax.random.fold_in(own_key, 6), dim), (blocks,), jnp.float32, least / len(pieces), top_value / len(pieces))
        return jnp.repeat(jnp.exp(steps), dims[dim] // blocks).reshape((-1,) + (1,) * (len(dims) - dim - 1))

    gain = one(*pieces[0])
    for cut in pieces[1:]:
        gain = gain * one(*cut)
    return gain


def profile(amount, total, reach, skew):
    portions = [(1 << 20) // math.isqrt(rank ** skew) + 1 for rank in range(2, amount + 1)]
    spare, given = total - reach - (amount - 1), [1] * (amount - 1)
    while spare > 0:
        free = [i for i in range(amount - 1) if given[i] < reach]
        pool, left = sum([portions[i] for i in free]), spare
        for i in free:
            more = min(reach - given[i], max(1, left * portions[i] // pool), spare)
            given[i] = given[i] + more
            spare = spare - more
    return np.array([reach] + given)


def uneven_parts(own_key, number_of, total, bound, lean):
    if number_of == 2:
        one = jax.random.randint(own_key, (), max(1, total - bound), min(bound, total - 1) + 1)
        return jnp.stack([one, total - one])
    tallies = jnp.asarray(profile(number_of, total, bound, lean), jnp.int32)
    couples = (number_of - 1) // 2
    donor, sink = tallies[1:1 + 2 * couples:2], tallies[2:2 + 2 * couples:2]
    room = jnp.minimum(donor - 1, bound - sink)
    passed = jax.random.randint(jax.random.fold_in(own_key, 1), (couples,), 0, 1 << 20) % (room + 1)
    tallies = tallies.at[1:1 + 2 * couples:2].set(donor - passed).at[2:2 + 2 * couples:2].set(sink + passed)
    return tallies[jax.random.permutation(jax.random.fold_in(own_key, 2), number_of)]


def scatter_about(rng, dims, width, bound, pieces=(), held_as=jnp.bfloat16):
    entries = width * jax.random.normal(rng, dims, jnp.float32)
    if pieces:
        entries = entries * block_scale(rng, dims, pieces, -0.22, 0.18)
    return jnp.clip(entries, -bound, bound).astype(held_as)


def heavy_noise(key, dims, width, reach, split, heavy, held_as=jnp.bfloat16):
    result = width * jax.random.normal(key, dims, jnp.float32)
    if split:
        result = result * block_scale(key, dims, split, -0.22, 0.18)
    return jnp.clip(raised(result, jax.random.fold_in(key, 3), *heavy), -reach, reach).astype(held_as)


def setup_inputs(seed: int = 0) -> dict:
    streams_of = jax.random.split(jax.random.key(seed), 7)
    return {
        "inputs": heavy_noise(streams_of[0], (D, SEQ), 1.0, 16.0, ((1, 64),), (1, 0, 64, 4.0)),
        "queries": draw_queries(jax.random.fold_in(streams_of[6], 71), 0),
        "keys": draw_keys(jax.random.fold_in(streams_of[6], 71), 0),
        "values": scatter_about(streams_of[3], (SEQ, KV_HEADS * HEAD_DIM), 1.0, 6.0, ((0, 64), (1, 4))),
        "grad_out": scatter_about(streams_of[4], (SEQ, Q_HEADS * HEAD_DIM), 1.0, 6.0, ((0, 64), (1, 4))),
        "doc_ids": jnp.searchsorted(jnp.cumsum(uneven_parts(streams_of[5], max(2, N_SEQ // 4), SEQ, 8 * TOK_DEV, 2)), jnp.arange(SEQ), side="right").astype(jnp.int32),
    }


SCALE = 168.0 ** -0.5
NEG = -1.0e30


def round_keep(value):
    return lax.optimization_barrier(value.astype(jnp.bfloat16)).astype(jnp.float32)


def reference(inputs, queries, keys, values, grad_out, doc_ids):
    group = Q_HEADS // KV_HEADS
    cols = KV_HEADS * HEAD_DIM
    span = WINDOW + TOK_DEV
    front = jnp.zeros((WINDOW, cols), jnp.bfloat16)
    key_pad = jnp.concatenate([front, keys], 0)
    value_pad = jnp.concatenate([front, values], 0)
    id_pad = jnp.concatenate([jnp.zeros((WINDOW,), jnp.int32), doc_ids.astype(jnp.int32)])
    offsets = jnp.arange(span, dtype=jnp.int32)
    rows_here = jnp.arange(TOK_DEV, dtype=jnp.int32)

    def block(carry, index):
        key_total, value_total = carry
        start = (index * TOK_DEV).astype(jnp.int32)
        q_blk = lax.dynamic_slice_in_dim(queries, start, TOK_DEV, 0).astype(jnp.float32).reshape(TOK_DEV, KV_HEADS, group, HEAD_DIM)
        o_blk = lax.dynamic_slice_in_dim(grad_out, start, TOK_DEV, 0).astype(jnp.float32).reshape(TOK_DEV, KV_HEADS, group, HEAD_DIM)
        k_blk = lax.dynamic_slice_in_dim(key_pad, start, span, 0).astype(jnp.float32).reshape(span, KV_HEADS, HEAD_DIM)
        v_blk = lax.dynamic_slice_in_dim(value_pad, start, span, 0).astype(jnp.float32).reshape(span, KV_HEADS, HEAD_DIM)
        q_pos = start + rows_here
        k_pos = start - WINDOW + offsets
        q_ids = lax.dynamic_slice_in_dim(doc_ids.astype(jnp.int32), start, TOK_DEV, 0)
        k_ids = lax.dynamic_slice_in_dim(id_pad, start, span, 0)
        allowed = (k_pos[None, :] <= q_pos[:, None]) & (k_pos[None, :] > q_pos[:, None] - WINDOW)
        allowed = allowed & (k_pos[None, :] >= 0) & (k_ids[None, :] == q_ids[:, None])
        scores = jnp.einsum('tkgd,skd->kgts', q_blk, k_blk) * SCALE
        scores = jnp.where(allowed, scores, NEG)
        top = jnp.max(scores, axis=-1, keepdims=True)
        expo = jnp.exp(scores - top)
        probs_f = expo / jnp.sum(expo, axis=-1, keepdims=True)
        probs = round_keep(probs_f)
        grad_probs = jnp.einsum('tkgd,skd->kgts', o_blk, v_blk)
        delta = jnp.sum(probs_f * grad_probs, axis=-1, keepdims=True)
        grad_scores = round_keep(SCALE * probs_f * (grad_probs - delta))
        grad_q = jnp.einsum('kgts,skd->tkgd', grad_scores, k_blk).reshape(TOK_DEV, Q_HEADS * HEAD_DIM).astype(jnp.bfloat16)
        grad_k = jnp.einsum('kgts,tkgd->skd', grad_scores, q_blk).reshape(span, cols)
        grad_v = jnp.einsum('kgts,tkgd->skd', probs, o_blk).reshape(span, cols)
        grad_k = jnp.concatenate([round_keep(grad_k[:WINDOW]), grad_k[WINDOW:]], 0)
        grad_v = jnp.concatenate([round_keep(grad_v[:WINDOW]), grad_v[WINDOW:]], 0)
        key_total = lax.dynamic_update_slice_in_dim(key_total, lax.dynamic_slice_in_dim(key_total, start, span, 0) + grad_k, start, 0)
        value_total = lax.dynamic_update_slice_in_dim(value_total, lax.dynamic_slice_in_dim(value_total, start, span, 0) + grad_v, start, 0)
        return (key_total, value_total), grad_q

    zeros = jnp.zeros((WINDOW + SEQ, cols), jnp.float32)
    (key_total, value_total), grad_q = lax.scan(block, (zeros, zeros), jnp.arange(SEQ // TOK_DEV, dtype=jnp.int32))
    grad_queries = grad_q.reshape(SEQ, Q_HEADS * HEAD_DIM)
    grad_keys = key_total[WINDOW:].astype(jnp.bfloat16)
    grad_values = value_total[WINDOW:].astype(jnp.bfloat16)
    grad_key_weight = jnp.dot(inputs, grad_keys, preferred_element_type=jnp.float32)
    grad_value_weight = jnp.dot(inputs, grad_values, preferred_element_type=jnp.float32)
    return grad_queries, grad_keys, grad_values, grad_key_weight, grad_value_weight
```

```python
import jax
import jax.numpy as jnp
from jax import lax
from jax.experimental import pallas as pl
from jax.experimental.pallas import tpu as pltpu
from jax.sharding import PartitionSpec as P

MESH = pl.DeviceIdType.MESH
SCALE = 168.0 ** -0.5
LOG2E = 1.4426950408889634
NEG = -1.0e30
T = 128
HALF = 512
WIN = 1536
SPAN = 1152
NZ = 8
F32 = jnp.float32
BF16 = jnp.bfloat16


def dims(lhs, rhs, lc, rc):
    return lax.dot_general(lhs, rhs, (((lc,), (rc,)), ((), ())), preferred_element_type=F32)


def kernel(
    x_ref, q_ref, k_ref, v_ref, o_ref, doc_ref,
    dq_out, dk_out, dv_out, wk_out, wv_out,
    qb, ob, kv, xb, acck, accv, lo_ref, dqs, ts, ps, t2s, tr2, gs, gb, pbuf, sdn, sup, rdn, rup,
    a_send, a_kv, a_q, z_send, z_recv, s_send, s_recv, x_send, x_recv, xs_sem,
    dq_send, dq_recv, t_sem, d_send, d_recv, dn_sem, up_sem,
):
    seq = lax.axis_index("seq")
    head = lax.axis_index("head")
    z = seq // 8
    i = seq % 8
    xl = head // 2
    core = head % 2
    own_half = i // 4
    lane = i % 4
    self_a = core == own_half

    def dev(zz, ii, cc):
        return (zz * 8 + ii, xl * 2 + cc)

    up = lax.rem(z + 1, NZ)
    down = lax.rem(z + NZ - 1, NZ)
    sibling = dev(z, i, 1 - core)
    above = dev(up, i, core)
    below = dev(down, i, core)

    def remote(src, dst, ssem, rsem, device):
        return pltpu.make_async_remote_copy(
            src_ref=src, dst_ref=dst, send_sem=ssem, recv_sem=rsem, device_id=device, device_id_type=MESH)

    def got(dst, sem):
        pltpu.make_async_copy(dst, dst, sem).wait()

    barrier = pltpu.get_barrier_semaphore()

    @pl.loop(1, 8)
    def _(step):
        for cc in range(2):
            pl.semaphore_signal(barrier, inc=1, device_id=dev(z, lax.rem(i + step, 8), cc), device_id_type=MESH)

    for other in (sibling, above, below):
        pl.semaphore_signal(barrier, inc=1, device_id=other, device_id_type=MESH)
    pl.semaphore_wait(barrier, 17)

    def a_parts(l):
        row = pl.multiple_of(lane * T, T)
        c1 = pl.multiple_of(l * T, T)
        c2 = pl.multiple_of(l * 2 * T, 2 * T)
        return (
            (k_ref.at[:, pl.ds(c1, T)], kv.at[pl.ds(1024 + row, T), pl.ds(0, T)], a_send.at[l, 0], a_kv.at[lane, 0]),
            (v_ref.at[:, pl.ds(c1, T)], kv.at[pl.ds(1024 + row, T), pl.ds(T, T)], a_send.at[l, 1], a_kv.at[lane, 1]),
            (q_ref.at[:, pl.ds(c2, 2 * T)], qb.at[pl.ds(row, T)], a_send.at[l, 2], a_q.at[lane, 0]),
            (o_ref.at[:, pl.ds(c2, 2 * T)], ob.at[pl.ds(row, T)], a_send.at[l, 3], a_q.at[lane, 1]),
        )

    def a_start(first, last):
        @pl.loop(0, 4)
        def _(step):
            l = lax.rem(lane + step, 4)
            mine = self_a & (l == lane)

            @pl.when(mine)
            def _():
                for src, dst, ssem, rsem in a_parts(l)[first:last]:
                    pltpu.make_async_copy(src, dst, rsem).start()

            @pl.when(jnp.logical_not(mine))
            def _():
                for src, dst, ssem, rsem in a_parts(l)[first:last]:
                    remote(src, dst, ssem, rsem, dev(z, 4 * core + l, own_half)).start()

    a_start(0, 2)
    a_start(2, 4)

    def x_part(ii):
        start = pl.multiple_of(84 * ii - 4 * (ii % 4), 16)
        zs = pl.ds(4 * core, 4)
        return x_ref.at[zs, pl.ds(start, 96), :], xb.at[zs, :, pl.ds(pl.multiple_of(i * T, T), T)]

    def x_copy(step):
        ii = lax.rem(i + step, 8)
        src, dst = x_part(ii)
        return remote(src, dst, x_send.at[step], x_recv.at[i], dev(z, ii, core))

    src, dst = x_part(i)
    pltpu.make_async_copy(src, dst, x_recv.at[i]).start()

    @pl.loop(1, 8)
    def _(step):
        x_copy(step).start()

    ids = doc_ref[pl.ds((2 * z + core) * 4, 4), :]
    table = doc_ref[...]
    begin = jnp.zeros((4, T), F32)
    for d in range(15):
        count = jnp.sum(jnp.where(table == d, 1.0, 0.0), axis=(0, 1), keepdims=True)
        begin = begin + jnp.where(ids > d, 1.0, 0.0) * count
    begin = begin.astype(jnp.int32) - (2 * z + core - 2) * HALF
    place = lax.broadcasted_iota(jnp.int32, (4, T), 1) + lax.broadcasted_iota(jnp.int32, (4, T), 0) * T
    lo_ref[0:4, :] = jnp.maximum(begin, place + 1)

    acck[...] = jnp.zeros_like(acck)
    accv[...] = jnp.zeros_like(accv)

    def rows(base, m):
        return pl.ds(pl.multiple_of(base + m * T, T), T)

    def z_copy(m):
        return remote(kv.at[rows(1024, m)], kv.at[rows(0, m)], z_send.at[m], z_recv.at[m], above)

    def s_copy(m):
        base = jnp.where(core == 0, 1024, 0)
        return remote(kv.at[rows(base, m)], kv.at[rows(512, m)], s_send.at[m], s_recv.at[m], sibling)

    @pl.loop(0, 4)
    def _(m):
        got(kv.at[rows(1024, m), pl.ds(0, T)], a_kv.at[m, 0])
        got(kv.at[rows(1024, m), pl.ds(T, T)], a_kv.at[m, 1])
        z_copy(m).start()

        @pl.when(core == 0)
        def _():
            s_copy(m).start()

    @pl.loop(0, 4)
    def _(m):
        z_copy(m).wait_recv()

        @pl.when(core == 1)
        def _():
            s_copy(m).start()

    @pl.loop(0, 4)
    def _(m):
        s_copy(m).wait_recv()
        got(qb.at[rows(0, m)], a_q.at[m, 0])
        got(ob.at[rows(0, m)], a_q.at[m, 1])

    @pl.loop(0, 4)
    def _(b):
        here = rows(0, b)
        span = pl.ds(pl.multiple_of(b * T, T), SPAN)
        q2 = jnp.concatenate([qb[here, 0:T], qb[here, T:2 * T]], 0)
        o2 = jnp.concatenate([ob[here, 0:T], ob[here, T:2 * T]], 0)
        kk = kv[span, 0:T]
        vv = kv[span, T:2 * T]
        scores = dims(kk, q2, 1, 1)
        spot = lax.broadcasted_iota(jnp.int32, (SPAN, 2 * T), 0)
        low = lo_ref[pl.ds(b, 1), :] - b * T
        low = jnp.concatenate([low, low], 1)
        high = 1024 + lax.broadcasted_iota(jnp.int32, (1, 2 * T), 1) % T
        scores = jnp.where((spot >= low) & (spot <= high), scores, NEG)
        top = jnp.max(scores, axis=0, keepdims=True)
        expo = jnp.exp2((scores - top) * (SCALE * LOG2E))
        probs = expo * (1.0 / jnp.sum(expo, axis=0, keepdims=True))
        grad_probs = dims(vv, o2, 1, 1)
        delta = jnp.sum(probs * grad_probs, axis=0, keepdims=True)
        grad_scores = (SCALE * probs * (grad_probs - delta)).astype(BF16)
        accv[span, :] += dims(probs.astype(BF16), o2, 1, 0)
        acck[span, :] += dims(grad_scores, q2, 1, 0)
        dq2 = dims(grad_scores, kk, 0, 0).astype(BF16)
        dqs[here, 0:T] = dq2[:T]
        dqs[here, T:2 * T] = dq2[T:]

    def ts_copy():
        return remote(ts, ps, t_sem.at[0], t_sem.at[1], sibling)

    def t2_copy():
        return remote(t2s, tr2, t_sem.at[2], t_sem.at[3], below)

    def put_terms():
        t2s[:, 0:T] = acck[0:512, :].astype(BF16)
        t2s[:, T:2 * T] = accv[0:512, :].astype(BF16)
        t2_copy().start()

    ts[:, 0:T] = acck[512:1024, :].astype(BF16)
    ts[:, T:2 * T] = accv[512:1024, :].astype(BF16)
    ts_copy().start()

    @pl.when(core == 0)
    def _():
        put_terms()

    def dq_copy(m):
        col = pl.ds(pl.multiple_of(lane * 2 * T, 2 * T), 2 * T)
        return dqs.at[rows(0, m)], dq_out.at[:, col], dq_send.at[m], dq_recv.at[lane], dev(z, 4 * core + m, own_half)

    @pl.loop(0, 4)
    def _(m):
        mine = self_a & (m == lane)
        src, dst, ssem, rsem, to = dq_copy(m)

        @pl.when(mine)
        def _():
            pltpu.make_async_copy(src, dst, rsem).start()

        @pl.when(jnp.logical_not(mine))
        def _():
            remote(src, dst, ssem, rsem, to).start()

    ts_copy().wait_recv()
    base = pl.ds(pl.multiple_of(jnp.where(core == 0, 1024, 0), 512), 512)
    acck[base, :] += ps[:, 0:T].astype(F32)
    accv[base, :] += ps[:, T:2 * T].astype(F32)

    @pl.when(core == 1)
    def _():
        put_terms()

    @pl.loop(0, 8)
    def _(j):
        zs = pl.ds(4 * core, 4)
        got(xb.at[zs, :, pl.ds(pl.multiple_of(j * T, T), T)], x_recv.at[j])

    def xs_copy():
        half = xb.at[pl.ds(4 * core, 4)]
        return remote(half, half, xs_sem.at[0], xs_sem.at[1], sibling)

    xs_copy().start()

    t2_copy().wait_recv()
    gs[0] = (accv[1024:1536, :] + tr2[:, T:2 * T].astype(F32)).astype(BF16)
    gs[1] = (acck[1024:1536, :] + tr2[:, 0:T].astype(F32)).astype(BF16)

    def d_copy(part, step):
        ii = lax.rem(i + step, 8)
        dst = gb.at[part, pl.ds(pl.multiple_of(core * HALF, HALF), HALF), pl.ds(pl.multiple_of(lane * T, T), T)]
        return gs.at[part], dst, d_send.at[part, step], d_recv.at[part, lane * 2 + core], dev(z, ii, own_half)

    for part in range(2):
        src, dst, ssem, rsem, to = d_copy(part, 0)

        @pl.when(self_a)
        def _():
            pltpu.make_async_copy(src, dst, rsem).start()

        @pl.when(jnp.logical_not(self_a))
        def _():
            remote(src, dst, ssem, rsem, to).start()

        @pl.loop(1, 8)
        def _(step):
            src, dst, ssem, rsem, to = d_copy(part, step)
            remote(src, dst, ssem, rsem, to).start()

    xs_copy().wait_recv()

    def dest(offset):
        return lax.rem(z + offset + NZ, NZ)

    def long_copy(part, k):
        to = below if part == 0 else above
        return remote(sdn.at[part, k], rdn.at[part, k], dn_sem.at[0, part, k], dn_sem.at[1, part, k], to)

    def short_copy(part, k):
        to = above if part == 0 else below
        return remote(sup.at[part, k], rup.at[part, k], up_sem.at[0, part, k], up_sem.at[1, part, k], to)

    def sign(part):
        return -1 if part == 0 else 1

    def ring(part, k):
        far = dest(sign(part) * (4 - k))
        value = pbuf[part, far]
        if k > 0:
            long_copy(part, k - 1).wait_recv()
            value = value + rdn[part, k - 1].astype(F32)
        sdn[part, k] = value.astype(BF16)
        long_copy(part, k).start()
        if k < 3:
            near = dest(-sign(part) * (3 - k))
            value = pbuf[part, near]
            if k > 0:
                short_copy(part, k - 1).wait_recv()
                value = value + rup[part, k - 1].astype(F32)
            sup[part, k] = value.astype(BF16)
            short_copy(part, k).start()

    for part in range(2):
        @pl.loop(0, 8)
        def _(n):
            dst = gb.at[part, pl.ds(pl.multiple_of((n % 2) * HALF, HALF), HALF),
                        pl.ds(pl.multiple_of((n // 2) * T, T), T)]
            got(dst, d_recv.at[part, n])

        @pl.loop(0, 4)
        def _(n):
            lhs = xb[pl.ds(2 * n, 2)].reshape(192, 1024)
            pbuf[part, pl.ds(2 * n, 2)] = jnp.dot(lhs, gb[part], preferred_element_type=F32).reshape(2, 96, 512)

        ring(part, 0)

    mine = pl.ds(pl.multiple_of(i * T, T), T)
    dv_out[...] = gb[0, mine, :]
    dk_out[...] = gb[1, mine, :]

    for k in range(1, 4):
        for part in range(2):
            ring(part, k)

    offset = 4 * (i % 4)
    for part in range(2):
        long_copy(part, 3).wait_recv()
        short_copy(part, 2).wait_recv()
        total = pbuf[part, z] + rdn[part, 3].astype(F32) + rup[part, 2].astype(F32)
        out = wv_out if part == 0 else wk_out
        out[...] = pltpu.roll(total, lax.rem(96 - offset, 96), 0)[:84]

    @pl.loop(0, 4)
    def _(l):
        got(dq_out.at[:, pl.ds(pl.multiple_of(l * 2 * T, 2 * T), 2 * T)], dq_recv.at[l])

    @pl.loop(0, 4)
    def _(m):
        z_copy(m).wait_send()
        s_copy(m).wait_send()
        src, dst, ssem, rsem, to = dq_copy(m)

        @pl.when(jnp.logical_not(self_a & (m == lane)))
        def _():
            for src_a, dst_a, ssem_a, rsem_a in a_parts(m):
                remote(src_a, dst_a, ssem_a, rsem_a, dev(z, 4 * core + m, own_half)).wait_send()
            remote(src, dst, ssem, rsem, to).wait_send()

    ts_copy().wait_send()
    t2_copy().wait_send()
    xs_copy().wait_send()

    @pl.loop(1, 8)
    def _(step):
        x_copy(step).wait_send()

    for part in range(2):
        src, dst, ssem, rsem, to = d_copy(part, 0)

        @pl.when(jnp.logical_not(self_a))
        def _():
            remote(src, dst, ssem, rsem, to).wait_send()

        @pl.loop(1, 8)
        def _(step):
            src, dst, ssem, rsem, to = d_copy(part, step)
            remote(src, dst, ssem, rsem, to).wait_send()

        for k in range(4):
            long_copy(part, k).wait_send()
        for k in range(3):
            short_copy(part, k).wait_send()


def local(inputs, queries, keys, values, grad_out, doc_ids):
    x = inputs.reshape(8, 672, 128)
    docs = doc_ids.reshape(64, 128)
    any_space = pl.BlockSpec(memory_space=pl.ANY)
    vmem = pl.BlockSpec(memory_space=pltpu.VMEM)
    dma = pltpu.SemaphoreType.DMA
    shape = jax.ShapeDtypeStruct
    return tuple(pl.pallas_call(
        kernel,
        name="window_backward",
        out_shape=(
            shape((T, 1024), BF16), shape((T, 512), BF16), shape((T, 512), BF16),
            shape((84, 512), F32), shape((84, 512), F32)),
        in_specs=[any_space] * 5 + [vmem],
        out_specs=(vmem,) * 5,
        scratch_shapes=[
            pltpu.VMEM((512, 256), BF16), pltpu.VMEM((512, 256), BF16), pltpu.VMEM((WIN, 256), BF16),
            pltpu.VMEM((8, 96, 1024), BF16), pltpu.VMEM((WIN, T), F32), pltpu.VMEM((WIN, T), F32),
            pltpu.VMEM((8, T), jnp.int32), pltpu.VMEM((512, 256), BF16),
            pltpu.VMEM((512, 256), BF16), pltpu.VMEM((512, 256), BF16), pltpu.VMEM((512, 256), BF16),
            pltpu.VMEM((512, 256), BF16), pltpu.VMEM((2, 512, T), BF16), pltpu.VMEM((2, 1024, 512), BF16),
            pltpu.VMEM((2, 8, 96, 512), F32),
            pltpu.VMEM((2, 4, 96, 512), BF16), pltpu.VMEM((2, 3, 96, 512), BF16),
            pltpu.VMEM((2, 4, 96, 512), BF16), pltpu.VMEM((2, 3, 96, 512), BF16),
            dma((4, 4)), dma((4, 2)), dma((4, 2)), dma((4,)), dma((4,)), dma((4,)), dma((4,)), dma((8,)), dma((8,)),
            dma((2,)), dma((4,)), dma((4,)), dma((4,)), dma((2, 8)), dma((2, 8)), dma((2, 2, 4)), dma((2, 2, 3)),
        ],
        compiler_params=pltpu.CompilerParams(
            collective_id=0, has_side_effects=True, vmem_limit_bytes=48 << 20),
        cost_estimate=pl.CostEstimate(flops=3_000_000_000, bytes_accessed=12_000_000, transcendentals=1_200_000),
    )(x, queries, keys, values, grad_out, docs))


def solution(mesh):
    return jax.shard_map(
        local,
        mesh=mesh,
        in_specs=(P(None, "seq"), P("seq", "head"), P("seq", "head"), P("seq", "head"), P("seq", "head"), P()),
        out_specs=(P("seq", "head"),) * 5,
        check_vma=False,
    )
```

```python
import jax
import jax.numpy as jnp
from jax import lax
from jax.experimental import pallas as pl
from jax.experimental.pallas import tpu as pltpu
from jax.sharding import PartitionSpec as P

MESH = pl.DeviceIdType.MESH
SCALE = 168.0 ** -0.5
LOG2E = 1.4426950408889634
NEG = -1.0e30
T = 128
HALF = 512
WIN = 1536
SPAN = 1152
NZ = 8
F32 = jnp.float32
BF16 = jnp.bfloat16


def dims(lhs, rhs, lc, rc):
    return lax.dot_general(lhs, rhs, (((lc,), (rc,)), ((), ())), preferred_element_type=F32)


def kernel(
    x_ref, q_ref, k_ref, v_ref, o_ref, doc_hbm,
    dq_out, dk_out, dv_out, wk_out, wv_out,
    qb, ob, kv, xb, acck, accv, lo_ref, dqs, t1s, tr1, t2s, tr2, gs, gb, pbuf, sdn, sup, rdn, rup, doc_ref, fin, precv,
    a_send, a_kv, a_q, z_send, z_recv, s_send, s_recv, x_send, x_recv, xs_sem,
    dq_send, dq_recv, t1_sem, t2_sem, d_send, d_recv, f_send, dn_send, dn_recv, up_send, up_recv, doc_sem, out_sem, g_send, g_recv, p_sem,
    xf_send, xf_recv,
):
    seq = lax.axis_index("seq")
    head = lax.axis_index("head")
    z = seq // 8
    i = seq % 8
    xl = head // 2
    core = head % 2
    own_half = i // 4
    lane = i % 4
    self_a = core == own_half
    y = i // 2
    xh = i % 2

    def dev(zz, ii, cc):
        return (zz * 8 + ii, xl * 2 + cc)

    up = lax.rem(z + 1, NZ)
    down = lax.rem(z + NZ - 1, NZ)
    sibling = dev(z, i, 1 - core)
    above = dev(up, i, core)
    below = dev(down, i, core)

    def remote(src, dst, ssem, rsem, device):
        return pltpu.make_async_remote_copy(
            src_ref=src, dst_ref=dst, send_sem=ssem, recv_sem=rsem, device_id=device, device_id_type=MESH)

    def got(dst, sem):
        pltpu.make_async_copy(dst, dst, sem).wait()

    docs = pltpu.make_async_copy(doc_hbm, doc_ref, doc_sem)
    docs.start()
    barrier = pltpu.get_barrier_semaphore()

    @pl.loop(1, 8)
    def _(step):
        for cc in range(2):
            pl.semaphore_signal(barrier, inc=1, device_id=dev(z, lax.rem(i + step, 8), cc), device_id_type=MESH)

    across = dev(jnp.where(core == 0, down, up), i, 1 - core)
    flip = i + 1 - 2 * xh
    opposite = (z * 8 + flip, (1 - xl) * 2 + core)
    for other in (sibling, above, below, across, opposite, dev(up, flip, core), dev(down, flip, core)):
        pl.semaphore_signal(barrier, inc=1, device_id=other, device_id_type=MESH)
    pl.semaphore_wait(barrier, 21)

    def a_parts(l):
        row = pl.multiple_of(lane * T, T)
        c1 = pl.multiple_of(l * T, T)
        c2 = pl.multiple_of(l * 2 * T, 2 * T)
        return (
            (k_ref.at[:, pl.ds(c1, T)], kv.at[pl.ds(1024 + row, T), pl.ds(0, T)], a_send.at[l, 0], a_kv.at[lane, 0]),
            (v_ref.at[:, pl.ds(c1, T)], kv.at[pl.ds(1024 + row, T), pl.ds(T, T)], a_send.at[l, 1], a_kv.at[lane, 1]),
            (q_ref.at[:, pl.ds(c2, 2 * T)], qb.at[pl.ds(row, T)], a_send.at[l, 2], a_q.at[lane, 0]),
            (o_ref.at[:, pl.ds(c2, 2 * T)], ob.at[pl.ds(row, T)], a_send.at[l, 3], a_q.at[lane, 1]),
        )

    def a_start(first, last):
        @pl.loop(0, 4)
        def _(step):
            l = lax.rem(lane + step, 4)
            mine = self_a & (l == lane)

            @pl.when(mine)
            def _():
                for src, dst, ssem, rsem in a_parts(l)[first:last]:
                    pltpu.make_async_copy(src, dst, rsem).start()

            @pl.when(jnp.logical_not(mine))
            def _():
                for src, dst, ssem, rsem in a_parts(l)[first:last]:
                    remote(src, dst, ssem, rsem, dev(z, 4 * core + l, own_half)).start()

    a_start(0, 2)
    a_start(2, 4)

    def x_part(yy, sub):
        row = 2 * yy + sub
        start = pl.multiple_of(84 * row - 4 * (row % 4), 16)
        zs = pl.ds(4 * core, 4)
        return x_ref.at[zs, pl.ds(start, 96), :], xb.at[sub, zs, :, pl.ds(pl.multiple_of(i * T, T), T)]

    def x_copy(step, sub):
        yy = lax.rem(y + step, 4)
        src, dst = x_part(yy, sub)
        return remote(src, dst, x_send.at[step, sub], x_recv.at[y, sub], dev(z, yy * 2 + xh, core))

    def x_start():
        for sub in range(2):
            src, dst = x_part(y, sub)
            pltpu.make_async_copy(src, dst, x_recv.at[y, sub]).start()

        @pl.loop(1, 4)
        def _(step):
            for sub in range(2):
                x_copy(step, sub).start()

    def x_tokens(j):
        return pl.ds(pl.multiple_of(j * T, T), T)

    def x_across(ys):
        piece = xb.at[:, pl.ds(4 * core, 4), :, x_tokens(ys * 2 + xh)]
        return remote(piece, piece, xf_send.at[ys], xf_recv.at[ys], opposite)

    def x_forward(step):
        ys = lax.rem(y + step, 4)
        for sub in range(2):
            got(xb.at[sub, pl.ds(4 * core, 4), :, x_tokens(ys * 2 + xh)], x_recv.at[ys, sub])
        x_across(ys).start()

    docs.wait()
    ids = doc_ref[pl.ds((2 * z + core) * 4, 4), :]
    table = doc_ref[...]
    begin = jnp.zeros((4, T), F32)
    for d in range(15):
        count = jnp.sum(jnp.where(table == d, 1.0, 0.0), axis=(0, 1), keepdims=True)
        begin = begin + jnp.where(ids > d, 1.0, 0.0) * count
    begin = begin.astype(jnp.int32) - (2 * z + core - 2) * HALF
    place = lax.broadcasted_iota(jnp.int32, (4, T), 1) + lax.broadcasted_iota(jnp.int32, (4, T), 0) * T
    lo_ref[0:4, :] = jnp.maximum(begin, place + 1)

    acck[...] = jnp.zeros_like(acck)
    accv[...] = jnp.zeros_like(accv)

    def rows(base, m):
        return pl.ds(pl.multiple_of(base + m * T, T), T)

    def z_copy(m):
        return remote(kv.at[rows(1024, m)], kv.at[rows(0, m)], z_send.at[m], z_recv.at[m], above)

    def s_copy(m):
        base = jnp.where(core == 0, 1024, 0)
        return remote(kv.at[rows(base, m)], kv.at[rows(512, m)], s_send.at[m], s_recv.at[m], sibling)

    @pl.loop(0, 4)
    def _(m):
        got(kv.at[rows(1024, m), pl.ds(0, T)], a_kv.at[m, 0])
        got(kv.at[rows(1024, m), pl.ds(T, T)], a_kv.at[m, 1])
        z_copy(m).start()

        @pl.when(core == 0)
        def _():
            s_copy(m).start()

    x_start()

    @pl.loop(0, 4)
    def _(m):
        z_copy(m).wait_recv()

        @pl.when(core == 1)
        def _():
            s_copy(m).start()

    @pl.loop(0, 4)
    def _(m):
        s_copy(m).wait_recv()
        got(qb.at[rows(0, m)], a_q.at[m, 0])
        got(ob.at[rows(0, m)], a_q.at[m, 1])

    def t2_copy(b):
        return remote(t2s.at[rows(0, b)], tr2.at[rows(0, b)], t2_sem.at[0, b], t2_sem.at[1, b], below)

    def dq_copy(m):
        col = pl.ds(pl.multiple_of(lane * 2 * T, 2 * T), 2 * T)
        return dqs.at[rows(0, m)], dq_out.at[:, col], dq_send.at[m], dq_recv.at[lane], dev(z, 4 * core + m, own_half)

    @pl.loop(0, 4)
    def _(b):
        here = rows(0, b)
        span = pl.ds(pl.multiple_of(b * T, T), SPAN)
        q2 = jnp.concatenate([qb[here, 0:T], qb[here, T:2 * T]], 0)
        o2 = jnp.concatenate([ob[here, 0:T], ob[here, T:2 * T]], 0)
        kk = kv[span, 0:T]
        vv = kv[span, T:2 * T]
        scores = dims(kk, q2, 1, 1)
        x_forward(b)
        spot = lax.broadcasted_iota(jnp.int32, (SPAN, 2 * T), 0)
        low = lo_ref[pl.ds(b, 1), :] - b * T
        low = jnp.concatenate([low, low], 1)
        high = 1024 + lax.broadcasted_iota(jnp.int32, (1, 2 * T), 1) % T
        scores = jnp.where((spot >= low) & (spot <= high), scores, NEG)
        top = jnp.max(scores, axis=0, keepdims=True)
        expo = jnp.exp2((scores - top) * (SCALE * LOG2E))
        probs = expo * (1.0 / jnp.sum(expo, axis=0, keepdims=True))
        grad_probs = dims(vv, o2, 1, 1)
        delta = jnp.sum(probs * grad_probs, axis=0, keepdims=True)
        grad_scores = (SCALE * probs * (grad_probs - delta)).astype(BF16)
        accv[span, :] += dims(probs.astype(BF16), o2, 1, 0)
        acck[span, :] += dims(grad_scores, q2, 1, 0)
        t2s[here, 0:T] = acck[here, :].astype(BF16)
        t2s[here, T:2 * T] = accv[here, :].astype(BF16)
        t2_copy(b).start()
        dq2 = dims(grad_scores, kk, 0, 0).astype(BF16)
        dqs[here, 0:T] = dq2[:T]
        dqs[here, T:2 * T] = dq2[T:]
        mine = self_a & (b == lane)
        src, dst, ssem, rsem, to = dq_copy(b)

        @pl.when(mine)
        def _():
            pltpu.make_async_copy(src, dst, rsem).start()

        @pl.when(jnp.logical_not(mine))
        def _():
            remote(src, dst, ssem, rsem, to).start()

    owner = dev(jnp.where(core == 0, down, z), i, 1 - core)

    def t1_copy(part):
        return remote(t1s.at[part], tr1.at[part], t1_sem.at[0, part], t1_sem.at[1, part], owner)

    for part, total in enumerate((accv, acck)):
        t1s[part] = total[512:1024, :].astype(BF16)
        t1_copy(part).start()

    @pl.loop(0, 4)
    def _(b):
        t2_copy(b).wait_recv()

    right = lax.rem(y + 1, 4) * 2 + xh
    left = lax.rem(y + 3, 4) * 2 + xh

    def block(part, u, a, h):
        return gb.at[part, pl.ds(pl.multiple_of(a * HALF + h * 256, 256), 256), pl.ds(pl.multiple_of(u * T, T), T)]

    def d_copy(part, n, h):
        to = dev(z, (right, left, i)[n], own_half)
        return (gs.at[part, pl.ds(h * 256, 256)], block(part, y % 2, core, h), d_send.at[part, n, h],
                d_recv.at[part, (y % 2) * 4 + core * 2 + h], to)

    def forward(part, u, a, h):
        piece = block(part, u, a, h)
        n = u * 4 + a * 2 + h
        return remote(piece, piece, f_send.at[part, n], d_recv.at[part, n], dev(z, jnp.where(h == 0, right, left), core))

    def arrived(part, u, a, h):
        got(block(part, u, a, h), d_recv.at[part, u * 4 + a * 2 + h])

    def steps_from(u):
        return lax.rem(y - 2 * core - u + 8, 4)

    def first_send(part):
        for h in range(2):
            for n in range(2):
                src, dst, ssem, rsem, to = d_copy(part, n, (h + n) % 2)
                remote(src, dst, ssem, rsem, to).start()
        for h in range(2):
            src, dst, ssem, rsem, to = d_copy(part, 2, h)

            @pl.when(self_a)
            def _():
                pltpu.make_async_copy(src, dst, rsem).start()

            @pl.when(jnp.logical_not(self_a))
            def _():
                remote(src, dst, ssem, rsem, to).start()

    def forward_side(part):
        @pl.loop(0, 4)
        def _(e):
            u, a = e // 2, e % 2
            steps = steps_from(u)

            @pl.when((steps == 1) | (steps == 3))
            def _():
                h = jnp.where(steps == 1, 0, 1)
                arrived(part, u, a, h)
                forward(part, u, a, h).start()

    def gathered(part):
        @pl.loop(0, 4)
        def _(e):
            u, a = e // 2, e % 2
            steps = steps_from(u)

            @pl.when((steps == 2) | (steps == 0))
            def _():
                arrived(part, u, a, 0)
                arrived(part, u, a, 1)

            @pl.when((steps == 1) | (steps == 3))
            def _():
                arrived(part, u, a, jnp.where(steps == 1, 1, 0))

    def sent(part):
        for n in range(2):
            for h in range(2):
                src, dst, ssem, rsem, to = d_copy(part, n, h)
                remote(src, dst, ssem, rsem, to).wait_send()

        @pl.when(jnp.logical_not(self_a))
        def _():
            for h in range(2):
                src, dst, ssem, rsem, to = d_copy(part, 2, h)
                remote(src, dst, ssem, rsem, to).wait_send()

        @pl.loop(0, 4)
        def _(e):
            u, a = e // 2, e % 2
            steps = steps_from(u)

            @pl.when((steps == 1) | (steps == 3))
            def _():
                forward(part, u, a, jnp.where(steps == 1, 0, 1)).wait_send()

    def g_copy(part, m):
        col = pl.ds(pl.multiple_of(lane * T, T), T)
        return (gs.at[part, rows(0, m)], (dv_out, dk_out)[part].at[:, col], g_send.at[part, m], g_recv.at[part, lane],
                dev(z, 4 * core + m, own_half))

    def token_send(part):
        @pl.loop(0, 4)
        def _(m):
            mine = self_a & (m == lane)
            src, dst, ssem, rsem, to = g_copy(part, m)

            @pl.when(mine)
            def _():
                pltpu.make_async_copy(src, dst, rsem).start()

            @pl.when(jnp.logical_not(mine))
            def _():
                remote(src, dst, ssem, rsem, to).start()

    def token_wait(part):
        @pl.loop(0, 4)
        def _(m):
            got((dv_out, dk_out)[part].at[:, pl.ds(pl.multiple_of(m * T, T), T)], g_recv.at[part, m])
            src, dst, ssem, rsem, to = g_copy(part, m)

            @pl.when(jnp.logical_not(self_a & (m == lane)))
            def _():
                remote(src, dst, ssem, rsem, to).wait_send()

    for part, total in enumerate((accv, acck)):
        t1_copy(part).wait_recv()
        cols = pl.ds((1 - part) * T, T)
        gs[part] = (total[1024:1536, :] + tr1[part].astype(F32) + tr2[:, cols].astype(F32)).astype(BF16)
        first_send(part)

    @pl.loop(0, 4)
    def _(ys):
        got(xb.at[:, pl.ds(4 * core, 4), :, x_tokens(ys * 2 + 1 - xh)], xf_recv.at[ys])

    def xs_copy():
        half = xb.at[:, pl.ds(4 * core, 4)]
        return remote(half, half, xs_sem.at[0], xs_sem.at[1], sibling)

    xs_copy().start()

    def dest(offset):
        return lax.rem(z + offset + NZ, NZ)

    def long_copy(part, sub, h, k):
        slot, ii = (xh, (i // 2) * 2 + sub) if k == 3 else (sub, i)
        return remote(sdn.at[part, sub, h, k], rdn.at[part, slot, h, k], dn_send.at[part, sub, h, k],
                      dn_recv.at[part, slot, h, k], dev(down if sub == 0 else up, ii, core))

    def short_copy(part, sub, h, k):
        slot, ii = (xh, (i // 2) * 2 + sub) if k == 2 else (sub, i)
        return remote(sup.at[part, sub, h, k], rup.at[part, slot, h, k], up_send.at[part, sub, h, k],
                      up_recv.at[part, slot, h, k], dev(up if sub == 0 else down, ii, core))

    def ring(part, k):
        for h in range(2):
            lines = slice(h * 48, h * 48 + 48)
            for sub in range(2):
                way = -1 if sub == 0 else 1
                value = pbuf[part, sub, dest(way * (4 - k)), lines]
                if k > 0:
                    got(rdn.at[part, sub, h, k - 1], dn_recv.at[part, sub, h, k - 1])
                    value = value + rdn[part, sub, h, k - 1].astype(F32)
                sdn[part, sub, h, k] = value.astype(BF16)
                long_copy(part, sub, h, k).start()
            if k < 3:
                for sub in range(2):
                    way = -1 if sub == 0 else 1
                    value = pbuf[part, sub, dest(-way * (3 - k)), lines]
                    if k > 0:
                        got(rup.at[part, sub, h, k - 1], up_recv.at[part, sub, h, k - 1])
                        value = value + rup[part, sub, h, k - 1].astype(F32)
                    sup[part, sub, h, k] = value.astype(BF16)
                    short_copy(part, sub, h, k).start()

    def product(part):
        @pl.loop(0, 4)
        def _(n):
            at = pl.ds((n % 2) * 4, 4)
            lhs = xb[n // 2, at].reshape(384, 1024)
            pbuf[part, n // 2, at] = jnp.dot(lhs, gb[part], preferred_element_type=F32).reshape(4, 96, 256)

    def p_copy(part):
        return remote(pbuf.at[part, 1 - xh, z], precv.at[part], p_sem.at[0, part], p_sem.at[1, part], dev(z, flip, core))

    offset = 4 * (i % 4)

    def weight_copy(part):
        return pltpu.make_async_copy(fin.at[part], (wv_out, wk_out)[part], out_sem.at[part])

    def finish(part):
        p_copy(part).wait_recv()
        for s in range(2):
            pieces = []
            for h in range(2):
                got(rdn.at[part, s, h, 3], dn_recv.at[part, s, h, 3])
                got(rup.at[part, s, h, 2], up_recv.at[part, s, h, 2])
                pieces.append(rdn[part, s, h, 3].astype(F32) + rup[part, s, h, 2].astype(F32))
            total = jnp.concatenate(pieces, 0) + jnp.where(xh == s, pbuf[part, s, z], precv[part])
            total = pltpu.roll(total, lax.rem(96 - offset, 96), 0)
            for u in range(2):
                fin[part, :, (u * 2 + s) * T:(u * 2 + s + 1) * T] = total[:84, u * T:(u + 1) * T]
        weight_copy(part).start()

    forward_side(0)
    forward_side(1)
    token_send(0)
    token_send(1)
    gathered(0)
    xs_copy().wait_recv()
    product(0)
    ring(0, 0)
    p_copy(0).start()
    ring(0, 1)
    gathered(1)
    product(1)
    ring(1, 0)
    p_copy(1).start()
    ring(0, 2)
    ring(1, 1)
    ring(0, 3)
    ring(1, 2)
    ring(1, 3)
    finish(0)
    finish(1)
    token_wait(0)
    token_wait(1)

    @pl.loop(0, 4)
    def _(l):
        got(dq_out.at[:, pl.ds(pl.multiple_of(l * 2 * T, 2 * T), 2 * T)], dq_recv.at[l])

    @pl.loop(0, 4)
    def _(m):
        z_copy(m).wait_send()
        s_copy(m).wait_send()
        src, dst, ssem, rsem, to = dq_copy(m)

        @pl.when(jnp.logical_not(self_a & (m == lane)))
        def _():
            for src_a, dst_a, ssem_a, rsem_a in a_parts(m):
                remote(src_a, dst_a, ssem_a, rsem_a, dev(z, 4 * core + m, own_half)).wait_send()
            remote(src, dst, ssem, rsem, to).wait_send()

    @pl.loop(0, 4)
    def _(b):
        t2_copy(b).wait_send()

    xs_copy().wait_send()

    @pl.loop(0, 4)
    def _(ys):
        x_across(ys).wait_send()

    @pl.loop(1, 4)
    def _(step):
        for sub in range(2):
            x_copy(step, sub).wait_send()

    for part in range(2):
        t1_copy(part).wait_send()
        sent(part)
        weight_copy(part).wait()
        p_copy(part).wait_send()
        for sub in range(2):
            for h in range(2):
                for k in range(4):
                    long_copy(part, sub, h, k).wait_send()
                for k in range(3):
                    short_copy(part, sub, h, k).wait_send()


def copies(*refs):
    count = 5
    inputs, outputs, held, sem = refs[:count], refs[count:2 * count], refs[2 * count:3 * count], refs[-1]
    loads = [pltpu.make_async_copy(inputs[n], held[n], sem.at[0, n]) for n in range(count)]
    stores = [pltpu.make_async_copy(held[n], outputs[n], sem.at[1, n]) for n in range(count)]
    for load in loads:
        load.start()
    for load, store in zip(loads, stores):
        load.wait()
        store.start()
    for store in stores:
        store.wait()


def local(inputs, queries, keys, values, grad_out, doc_ids):
    x = inputs.reshape(8, 672, 128)
    docs = doc_ids.reshape(64, 128)
    anywhere = pl.BlockSpec(memory_space=pl.ANY)
    dma = pltpu.SemaphoreType.DMA
    shape = jax.ShapeDtypeStruct
    vmem = pltpu.VMEM
    outs = (
        shape((T, 1024), BF16), shape((T, 512), BF16), shape((T, 512), BF16), shape((84, 512), F32), shape((84, 512), F32))
    results = pl.pallas_call(
        kernel,
        name="window_backward",
        out_shape=outs,
        in_specs=[anywhere] * 6,
        out_specs=(anywhere,) * 5,
        scratch_shapes=[
            vmem((512, 256), BF16), vmem((512, 256), BF16), vmem((WIN, 256), BF16),
            vmem((2, 8, 96, 1024), BF16), vmem((WIN, T), F32), vmem((WIN, T), F32),
            vmem((8, T), jnp.int32), vmem((512, 256), BF16),
            vmem((2, 512, T), BF16), vmem((2, 512, T), BF16), vmem((512, 256), BF16), vmem((512, 256), BF16),
            vmem((2, 512, T), BF16), vmem((2, 1024, 256), BF16),
            vmem((2, 2, 8, 96, 256), F32),
            vmem((2, 2, 2, 4, 48, 256), BF16), vmem((2, 2, 2, 3, 48, 256), BF16),
            vmem((2, 2, 2, 4, 48, 256), BF16), vmem((2, 2, 2, 3, 48, 256), BF16), vmem((64, 128), jnp.int32), vmem((2, 84, 512), F32),
            vmem((2, 96, 256), F32),
            dma((4, 4)), dma((4, 2)), dma((4, 2)), dma((4,)), dma((4,)), dma((4,)), dma((4,)), dma((4, 2)), dma((4, 2)), dma((2,)),
            dma((4,)), dma((4,)), dma((2, 2)), dma((2, 4)), dma((2, 3, 2)), dma((2, 8)), dma((2, 8)),
            dma((2, 2, 2, 4)), dma((2, 2, 2, 4)), dma((2, 2, 2, 3)), dma((2, 2, 2, 3)), dma(()), dma((2,)), dma((2, 4)), dma((2, 4)),
            dma((2, 2)), dma((4,)), dma((4,)),
        ],
        compiler_params=pltpu.CompilerParams(
            collective_id=0, has_side_effects=True, vmem_limit_bytes=60 << 20),
        cost_estimate=pl.CostEstimate(flops=3_000_000_000, bytes_accessed=12_000_000, transcendentals=1_200_000),
    )(x, queries, keys, values, grad_out, docs)
    return tuple(pl.pallas_call(
        copies,
        name="results",
        out_shape=outs,
        in_specs=[anywhere] * 5,
        out_specs=(anywhere,) * 5,
        scratch_shapes=[vmem(o.shape, o.dtype) for o in outs] + [dma((2, 5))],
        compiler_params=pltpu.CompilerParams(vmem_limit_bytes=60 << 20),
    )(*results))


def solution(mesh):
    return jax.shard_map(
        local,
        mesh=mesh,
        in_specs=(P(None, "seq"), P("seq", "head"), P("seq", "head"), P("seq", "head"), P("seq", "head"), P()),
        out_specs=(P("seq", "head"),) * 5,
        check_vma=False,
    )
```

```python
import jax
import jax.numpy as jnp
from jax import lax
from jax.experimental import pallas as pl
from jax.experimental.pallas import tpu as pltpu
from jax.sharding import PartitionSpec as P

MESH = pl.DeviceIdType.MESH
SCALE = 168.0 ** -0.5
LOG2E = 1.4426950408889634
NEG = -1.0e30
T = 128
HALF = 512
WIN = 1536
SPAN = 1152
NZ = 8
F32 = jnp.float32
BF16 = jnp.bfloat16


def dims(lhs, rhs, lc, rc):
    return lax.dot_general(lhs, rhs, (((lc,), (rc,)), ((), ())), preferred_element_type=F32)


def kernel(
    x_ref, q_ref, k_ref, v_ref, o_ref, doc_hbm,
    dq_out, dk_out, dv_out, wk_out, wv_out,
    qb, ob, kv, xb, acck, accv, lo_ref, dqs, t1s, tr1, t2s, tr2, gs, gb, pbuf, sdn, sup, rdn, rup, doc_ref, fin, precv,
    a_send, a_kv, a_q, z_send, z_recv, s_send, s_recv, x_send, x_recv, xs_send, xs_recv,
    dq_send, dq_recv, t1_sem, t2_sem, d_send, d_recv, f_send, dn_send, dn_recv, up_send, up_recv, doc_sem, out_sem, g_send, g_recv, p_sem,
    xf_send, xf_recv, xg_send, xg_recv,
):
    seq = lax.axis_index("seq")
    head = lax.axis_index("head")
    z = seq // 8
    i = seq % 8
    xl = head // 2
    core = head % 2
    own_half = i // 4
    lane = i % 4
    self_a = core == own_half
    y = i // 2
    xh = i % 2

    def dev(zz, ii, cc):
        return (zz * 8 + ii, xl * 2 + cc)

    up = lax.rem(z + 1, NZ)
    down = lax.rem(z + NZ - 1, NZ)
    sibling = dev(z, i, 1 - core)
    above = dev(up, i, core)
    below = dev(down, i, core)

    def remote(src, dst, ssem, rsem, device):
        return pltpu.make_async_remote_copy(
            src_ref=src, dst_ref=dst, send_sem=ssem, recv_sem=rsem, device_id=device, device_id_type=MESH)

    def got(dst, sem):
        pltpu.make_async_copy(dst, dst, sem).wait()

    docs = pltpu.make_async_copy(doc_hbm, doc_ref, doc_sem)
    docs.start()
    barrier = pltpu.get_barrier_semaphore()

    @pl.loop(1, 8)
    def _(step):
        for cc in range(2):
            pl.semaphore_signal(barrier, inc=1, device_id=dev(z, lax.rem(i + step, 8), cc), device_id_type=MESH)

    across = dev(jnp.where(core == 0, down, up), i, 1 - core)
    flip = i + 1 - 2 * xh
    opposite = (z * 8 + flip, (1 - xl) * 2 + core)
    beside = (seq, (1 - xl) * 2 + core)
    for other in (sibling, above, below, across, opposite, beside, dev(up, flip, core), dev(down, flip, core)):
        pl.semaphore_signal(barrier, inc=1, device_id=other, device_id_type=MESH)
    pl.semaphore_wait(barrier, 22)

    def a_parts(l):
        row = pl.multiple_of(lane * T, T)
        c1 = pl.multiple_of(l * T, T)
        c2 = pl.multiple_of(l * 2 * T, 2 * T)
        return (
            (k_ref.at[:, pl.ds(c1, T)], kv.at[pl.ds(1024 + row, T), pl.ds(0, T)], a_send.at[l, 0], a_kv.at[lane, 0]),
            (v_ref.at[:, pl.ds(c1, T)], kv.at[pl.ds(1024 + row, T), pl.ds(T, T)], a_send.at[l, 1], a_kv.at[lane, 1]),
            (q_ref.at[:, pl.ds(c2, 2 * T)], qb.at[pl.ds(row, T)], a_send.at[l, 2], a_q.at[lane, 0]),
            (o_ref.at[:, pl.ds(c2, 2 * T)], ob.at[pl.ds(row, T)], a_send.at[l, 3], a_q.at[lane, 1]),
        )

    def a_start(first, last):
        @pl.loop(0, 4)
        def _(step):
            l = lax.rem(lane + step, 4)
            mine = self_a & (l == lane)

            @pl.when(mine)
            def _():
                for src, dst, ssem, rsem in a_parts(l)[first:last]:
                    pltpu.make_async_copy(src, dst, rsem).start()

            @pl.when(jnp.logical_not(mine))
            def _():
                for src, dst, ssem, rsem in a_parts(l)[first:last]:
                    remote(src, dst, ssem, rsem, dev(z, 4 * core + l, own_half)).start()

    a_start(0, 2)
    a_start(2, 4)

    zs = pl.ds(4 * core, 4)
    others = pl.ds(4 * (1 - core), 4)

    def x_part(yy, sub):
        row = 2 * yy + sub
        start = pl.multiple_of(84 * row - 4 * (row % 4), 16)
        return x_ref.at[zs, pl.ds(start, 96), :], xb.at[sub, i, zs]

    def x_copy(step, sub):
        yy = lax.rem(y + step, 4)
        src, dst = x_part(yy, sub)
        return remote(src, dst, x_send.at[step, sub], x_recv.at[y, sub], dev(z, yy * 2 + xh, core))

    def x_across_own():
        src, dst = x_part(y, xl)
        return remote(src, dst, xf_send.at[y], xf_recv.at[y], opposite)

    def x_across(ys):
        piece = xb.at[xl, ys * 2 + xh, zs]
        return remote(piece, piece, xf_send.at[ys], xf_recv.at[ys], opposite)

    def x_beside(ys):
        piece = xb.at[1 - xl, ys * 2 + 1 - xh, zs]
        return remote(piece, piece, xg_send.at[ys], xg_recv.at[ys], beside)

    def xs_own(ys):
        piece = xb.at[:, ys * 2 + xh, zs]
        return remote(piece, piece, xs_send.at[ys, 0], xs_recv.at[ys, 0], sibling)

    def xs_other(ys, s):
        piece = xb.at[1 - xl if s == 0 else xl, ys * 2 + 1 - xh, zs]
        return remote(piece, piece, xs_send.at[ys, 1 + s], xs_recv.at[ys, 1 + s], sibling)

    def near_first(b):
        return lax.rem(y + jnp.where(b < 2, b, 5 - b), 4)

    def x_start():
        for sub in range(2):
            src, dst = x_part(y, sub)
            pltpu.make_async_copy(src, dst, x_recv.at[y, sub]).start()

        x_across_own().start()

        @pl.loop(1, 4)
        def _(b):
            for sub in range(2):
                x_copy(jnp.where(b < 2, b, 5 - b), sub).start()

    def x_arrived(ys):
        for sub in range(2):
            got(xb.at[sub, ys * 2 + xh, zs], x_recv.at[ys, sub])
        xs_own(ys).start()

    def x_second(b):
        ys = near_first(b)
        got(xb.at[1 - xl, ys * 2 + 1 - xh, zs], xf_recv.at[ys])
        x_beside(ys).start()
        xs_other(ys, 0).start()

    def x_third(b):
        ys = near_first(b)
        got(xb.at[xl, ys * 2 + 1 - xh, zs], xg_recv.at[ys])
        xs_other(ys, 1).start()

    def x_complete():
        @pl.loop(0, 4)
        def _(ys):
            got(xb.at[:, ys * 2 + xh, others], xs_recv.at[ys, 0])
            got(xb.at[1 - xl, ys * 2 + 1 - xh, others], xs_recv.at[ys, 1])
            got(xb.at[xl, ys * 2 + 1 - xh, others], xs_recv.at[ys, 2])

    x_start()

    docs.wait()
    ids = doc_ref[pl.ds((2 * z + core) * 4, 4), :]
    table = doc_ref[...]
    begin = jnp.zeros((4, T), F32)
    for d in range(15):
        count = jnp.sum(jnp.where(table == d, 1.0, 0.0), axis=(0, 1), keepdims=True)
        begin = begin + jnp.where(ids > d, 1.0, 0.0) * count
    begin = begin.astype(jnp.int32) - (2 * z + core - 2) * HALF
    place = lax.broadcasted_iota(jnp.int32, (4, T), 1) + lax.broadcasted_iota(jnp.int32, (4, T), 0) * T
    lo_ref[0:4, :] = jnp.maximum(begin, place + 1)

    acck[...] = jnp.zeros_like(acck)
    accv[...] = jnp.zeros_like(accv)

    def rows(base, m):
        return pl.ds(pl.multiple_of(base + m * T, T), T)

    def z_copy(m):
        return remote(kv.at[rows(1024, m)], kv.at[rows(0, m)], z_send.at[m], z_recv.at[m], above)

    def s_copy(m):
        base = jnp.where(core == 0, 1024, 0)
        return remote(kv.at[rows(base, m)], kv.at[rows(512, m)], s_send.at[m], s_recv.at[m], sibling)

    @pl.loop(0, 4)
    def _(m):
        got(kv.at[rows(1024, m), pl.ds(0, T)], a_kv.at[m, 0])
        got(kv.at[rows(1024, m), pl.ds(T, T)], a_kv.at[m, 1])
        z_copy(m).start()

        @pl.when(core == 0)
        def _():
            s_copy(m).start()

    @pl.loop(0, 4)
    def _(m):
        z_copy(m).wait_recv()

        @pl.when(core == 1)
        def _():
            s_copy(m).start()

    @pl.loop(0, 4)
    def _(m):
        s_copy(m).wait_recv()
        got(qb.at[rows(0, m)], a_q.at[m, 0])
        got(ob.at[rows(0, m)], a_q.at[m, 1])

    def t2_copy(b):
        return remote(t2s.at[rows(0, b)], tr2.at[rows(0, b)], t2_sem.at[0, b], t2_sem.at[1, b], below)

    def dq_copy(m):
        col = pl.ds(pl.multiple_of(lane * 2 * T, 2 * T), 2 * T)
        return dqs.at[rows(0, m)], dq_out.at[:, col], dq_send.at[m], dq_recv.at[lane], dev(z, 4 * core + m, own_half)

    @pl.loop(0, 4)
    def _(b):
        here = rows(0, b)
        span = pl.ds(pl.multiple_of(b * T, T), SPAN)
        q2 = jnp.concatenate([qb[here, 0:T], qb[here, T:2 * T]], 0)
        o2 = jnp.concatenate([ob[here, 0:T], ob[here, T:2 * T]], 0)
        kk = kv[span, 0:T]
        vv = kv[span, T:2 * T]
        scores = dims(kk, q2, 1, 1)
        spot = lax.broadcasted_iota(jnp.int32, (SPAN, 2 * T), 0)
        low = lo_ref[pl.ds(b, 1), :] - b * T
        low = jnp.concatenate([low, low], 1)
        high = 1024 + lax.broadcasted_iota(jnp.int32, (1, 2 * T), 1) % T
        scores = jnp.where((spot >= low) & (spot <= high), scores, NEG)
        top = jnp.max(scores, axis=0, keepdims=True)
        expo = jnp.exp2((scores - top) * (SCALE * LOG2E))
        probs = expo * (1.0 / jnp.sum(expo, axis=0, keepdims=True))
        grad_probs = dims(vv, o2, 1, 1)
        delta = jnp.sum(probs * grad_probs, axis=0, keepdims=True)
        grad_scores = (SCALE * probs * (grad_probs - delta)).astype(BF16)
        accv[span, :] += dims(probs.astype(BF16), o2, 1, 0)
        acck[span, :] += dims(grad_scores, q2, 1, 0)
        t2s[here, 0:T] = acck[here, :].astype(BF16)
        t2s[here, T:2 * T] = accv[here, :].astype(BF16)
        t2_copy(b).start()
        dq2 = dims(grad_scores, kk, 0, 0).astype(BF16)
        dqs[here, 0:T] = dq2[:T]
        dqs[here, T:2 * T] = dq2[T:]
        mine = self_a & (b == lane)
        src, dst, ssem, rsem, to = dq_copy(b)

        @pl.when(mine)
        def _():
            pltpu.make_async_copy(src, dst, rsem).start()

        @pl.when(jnp.logical_not(mine))
        def _():
            remote(src, dst, ssem, rsem, to).start()

    owner = dev(jnp.where(core == 0, down, z), i, 1 - core)

    def t1_copy(part):
        return remote(t1s.at[part], tr1.at[part], t1_sem.at[0, part], t1_sem.at[1, part], owner)

    for part, total in enumerate((accv, acck)):
        t1s[part] = total[512:1024, :].astype(BF16)
        t1_copy(part).start()

    @pl.loop(1, 4)
    def _(b):
        ys = near_first(b)
        x_arrived(ys)
        x_across(ys).start()

    x_arrived(y)
    x_second(0)

    @pl.loop(0, 4)
    def _(b):
        t2_copy(b).wait_recv()

    right = lax.rem(y + 1, 4) * 2 + xh
    left = lax.rem(y + 3, 4) * 2 + xh

    def block(part, u, a, h):
        return gb.at[part, pl.ds(pl.multiple_of(a * HALF + h * 256, 256), 256), pl.ds(pl.multiple_of(u * T, T), T)]

    def d_copy(part, n, h):
        to = dev(z, (right, left, i)[n], own_half)
        return (gs.at[part, pl.ds(h * 256, 256)], block(part, y % 2, core, h), d_send.at[part, n, h],
                d_recv.at[part, (y % 2) * 4 + core * 2 + h], to)

    def forward(part, u, a, h):
        piece = block(part, u, a, h)
        n = u * 4 + a * 2 + h
        return remote(piece, piece, f_send.at[part, n], d_recv.at[part, n], dev(z, jnp.where(h == 0, right, left), core))

    def arrived(part, u, a, h):
        got(block(part, u, a, h), d_recv.at[part, u * 4 + a * 2 + h])

    def steps_from(u):
        return lax.rem(y - 2 * core - u + 8, 4)

    def first_send(part):
        for h in range(2):
            for n in range(2):
                src, dst, ssem, rsem, to = d_copy(part, n, (h + n) % 2)
                remote(src, dst, ssem, rsem, to).start()
        for h in range(2):
            src, dst, ssem, rsem, to = d_copy(part, 2, h)

            @pl.when(self_a)
            def _():
                pltpu.make_async_copy(src, dst, rsem).start()

            @pl.when(jnp.logical_not(self_a))
            def _():
                remote(src, dst, ssem, rsem, to).start()

    def forward_side(part):
        @pl.loop(0, 4)
        def _(e):
            u, a = e // 2, e % 2
            steps = steps_from(u)

            @pl.when((steps == 1) | (steps == 3))
            def _():
                h = jnp.where(steps == 1, 0, 1)
                arrived(part, u, a, h)
                forward(part, u, a, h).start()

    def gathered(part):
        @pl.loop(0, 4)
        def _(e):
            u, a = e // 2, e % 2
            steps = steps_from(u)

            @pl.when((steps == 2) | (steps == 0))
            def _():
                arrived(part, u, a, 0)
                arrived(part, u, a, 1)

            @pl.when((steps == 1) | (steps == 3))
            def _():
                arrived(part, u, a, jnp.where(steps == 1, 1, 0))

    def sent(part):
        for n in range(2):
            for h in range(2):
                src, dst, ssem, rsem, to = d_copy(part, n, h)
                remote(src, dst, ssem, rsem, to).wait_send()

        @pl.when(jnp.logical_not(self_a))
        def _():
            for h in range(2):
                src, dst, ssem, rsem, to = d_copy(part, 2, h)
                remote(src, dst, ssem, rsem, to).wait_send()

        @pl.loop(0, 4)
        def _(e):
            u, a = e // 2, e % 2
            steps = steps_from(u)

            @pl.when((steps == 1) | (steps == 3))
            def _():
                forward(part, u, a, jnp.where(steps == 1, 0, 1)).wait_send()

    def g_copy(part, m):
        col = pl.ds(pl.multiple_of(lane * T, T), T)
        return (gs.at[part, rows(0, m)], (dv_out, dk_out)[part].at[:, col], g_send.at[part, m], g_recv.at[part, lane],
                dev(z, 4 * core + m, own_half))

    def token_send(part):
        @pl.loop(0, 4)
        def _(m):
            mine = self_a & (m == lane)
            src, dst, ssem, rsem, to = g_copy(part, m)

            @pl.when(mine)
            def _():
                pltpu.make_async_copy(src, dst, rsem).start()

            @pl.when(jnp.logical_not(mine))
            def _():
                remote(src, dst, ssem, rsem, to).start()

    def token_wait(part):
        @pl.loop(0, 4)
        def _(m):
            got((dv_out, dk_out)[part].at[:, pl.ds(pl.multiple_of(m * T, T), T)], g_recv.at[part, m])
            src, dst, ssem, rsem, to = g_copy(part, m)

            @pl.when(jnp.logical_not(self_a & (m == lane)))
            def _():
                remote(src, dst, ssem, rsem, to).wait_send()

    for part, total in enumerate((accv, acck)):
        t1_copy(part).wait_recv()
        cols = pl.ds((1 - part) * T, T)
        gs[part] = (total[1024:1536, :] + tr1[part].astype(F32) + tr2[:, cols].astype(F32)).astype(BF16)
        first_send(part)

    @pl.loop(1, 4)
    def _(b):
        x_second(b)


    def dest(offset):
        return lax.rem(z + offset + NZ, NZ)

    def long_copy(part, sub, h, k):
        slot, ii = (xh, (i // 2) * 2 + sub) if k == 3 else (sub, i)
        return remote(sdn.at[part, sub, h, k], rdn.at[part, slot, h, k], dn_send.at[part, sub, h, k],
                      dn_recv.at[part, slot, h, k], dev(down if sub == 0 else up, ii, core))

    def short_copy(part, sub, h, k):
        slot, ii = (xh, (i // 2) * 2 + sub) if k == 2 else (sub, i)
        return remote(sup.at[part, sub, h, k], rup.at[part, slot, h, k], up_send.at[part, sub, h, k],
                      up_recv.at[part, slot, h, k], dev(up if sub == 0 else down, ii, core))

    def ring(part, k):
        for h in range(2):
            lines = slice(h * 48, h * 48 + 48)
            for sub in range(2):
                way = -1 if sub == 0 else 1
                value = pbuf[part, sub, dest(way * (4 - k)), lines]
                if k > 0:
                    got(rdn.at[part, sub, h, k - 1], dn_recv.at[part, sub, h, k - 1])
                    value = value + rdn[part, sub, h, k - 1].astype(F32)
                sdn[part, sub, h, k] = value.astype(BF16)
                long_copy(part, sub, h, k).start()
            if k < 3:
                for sub in range(2):
                    way = -1 if sub == 0 else 1
                    value = pbuf[part, sub, dest(-way * (3 - k)), lines]
                    if k > 0:
                        got(rup.at[part, sub, h, k - 1], up_recv.at[part, sub, h, k - 1])
                        value = value + rup[part, sub, h, k - 1].astype(F32)
                    sup[part, sub, h, k] = value.astype(BF16)
                    short_copy(part, sub, h, k).start()

    def product(part):
        @pl.loop(0, 4)
        def _(n):
            at = pl.ds((n % 2) * 4, 4)
            lhs = jnp.concatenate([xb[n // 2, j, at].reshape(384, T) for j in range(8)], 1)
            pbuf[part, n // 2, at] = jnp.dot(lhs, gb[part], preferred_element_type=F32).reshape(4, 96, 256)

    def p_copy(part):
        return remote(pbuf.at[part, 1 - xh, z], precv.at[part], p_sem.at[0, part], p_sem.at[1, part], dev(z, flip, core))

    offset = 4 * (i % 4)

    def weight_copy(part):
        return pltpu.make_async_copy(fin.at[part], (wv_out, wk_out)[part], out_sem.at[part])

    def finish(part):
        p_copy(part).wait_recv()
        for s in range(2):
            pieces = []
            for h in range(2):
                got(rdn.at[part, s, h, 3], dn_recv.at[part, s, h, 3])
                got(rup.at[part, s, h, 2], up_recv.at[part, s, h, 2])
                pieces.append(rdn[part, s, h, 3].astype(F32) + rup[part, s, h, 2].astype(F32))
            total = jnp.concatenate(pieces, 0) + jnp.where(xh == s, pbuf[part, s, z], precv[part])
            total = pltpu.roll(total, lax.rem(96 - offset, 96), 0)
            for u in range(2):
                fin[part, :, (u * 2 + s) * T:(u * 2 + s + 1) * T] = total[:84, u * T:(u + 1) * T]
        weight_copy(part).start()

    forward_side(0)
    forward_side(1)
    token_send(0)
    token_send(1)

    @pl.loop(0, 4)
    def _(b):
        x_third(b)

    gathered(0)
    x_complete()
    product(0)
    ring(0, 0)
    p_copy(0).start()
    ring(0, 1)
    gathered(1)
    product(1)
    ring(1, 0)
    p_copy(1).start()
    ring(0, 2)
    ring(1, 1)
    ring(0, 3)
    ring(1, 2)
    ring(1, 3)
    finish(0)
    finish(1)
    token_wait(0)
    token_wait(1)

    @pl.loop(0, 4)
    def _(l):
        got(dq_out.at[:, pl.ds(pl.multiple_of(l * 2 * T, 2 * T), 2 * T)], dq_recv.at[l])

    @pl.loop(0, 4)
    def _(m):
        z_copy(m).wait_send()
        s_copy(m).wait_send()
        src, dst, ssem, rsem, to = dq_copy(m)

        @pl.when(jnp.logical_not(self_a & (m == lane)))
        def _():
            for src_a, dst_a, ssem_a, rsem_a in a_parts(m):
                remote(src_a, dst_a, ssem_a, rsem_a, dev(z, 4 * core + m, own_half)).wait_send()
            remote(src, dst, ssem, rsem, to).wait_send()

    @pl.loop(0, 4)
    def _(b):
        t2_copy(b).wait_send()


    @pl.loop(0, 4)
    def _(ys):
        x_across(ys).wait_send()
        x_beside(ys).wait_send()
        xs_own(ys).wait_send()
        for s in range(2):
            xs_other(ys, s).wait_send()

    @pl.loop(1, 4)
    def _(step):
        for sub in range(2):
            x_copy(step, sub).wait_send()

    for part in range(2):
        t1_copy(part).wait_send()
        sent(part)
        weight_copy(part).wait()
        p_copy(part).wait_send()
        for sub in range(2):
            for h in range(2):
                for k in range(4):
                    long_copy(part, sub, h, k).wait_send()
                for k in range(3):
                    short_copy(part, sub, h, k).wait_send()


def copies(*refs):
    count = 5
    inputs, outputs, held, sem = refs[:count], refs[count:2 * count], refs[2 * count:3 * count], refs[-1]
    loads = [pltpu.make_async_copy(inputs[n], held[n], sem.at[0, n]) for n in range(count)]
    stores = [pltpu.make_async_copy(held[n], outputs[n], sem.at[1, n]) for n in range(count)]
    for load in loads:
        load.start()
    for load, store in zip(loads, stores):
        load.wait()
        store.start()
    for store in stores:
        store.wait()


def local(inputs, queries, keys, values, grad_out, doc_ids):
    x = inputs.reshape(8, 672, 128)
    docs = doc_ids.reshape(64, 128)
    anywhere = pl.BlockSpec(memory_space=pl.ANY)
    dma = pltpu.SemaphoreType.DMA
    shape = jax.ShapeDtypeStruct
    vmem = pltpu.VMEM
    outs = (
        shape((T, 1024), BF16), shape((T, 512), BF16), shape((T, 512), BF16), shape((84, 512), F32), shape((84, 512), F32))
    results = pl.pallas_call(
        kernel,
        name="window_backward",
        out_shape=outs,
        in_specs=[anywhere] * 6,
        out_specs=(anywhere,) * 5,
        scratch_shapes=[
            vmem((512, 256), BF16), vmem((512, 256), BF16), vmem((WIN, 256), BF16),
            vmem((2, 8, 8, 96, T), BF16), vmem((WIN, T), F32), vmem((WIN, T), F32),
            vmem((8, T), jnp.int32), vmem((512, 256), BF16),
            vmem((2, 512, T), BF16), vmem((2, 512, T), BF16), vmem((512, 256), BF16), vmem((512, 256), BF16),
            vmem((2, 512, T), BF16), vmem((2, 1024, 256), BF16),
            vmem((2, 2, 8, 96, 256), F32),
            vmem((2, 2, 2, 4, 48, 256), BF16), vmem((2, 2, 2, 3, 48, 256), BF16),
            vmem((2, 2, 2, 4, 48, 256), BF16), vmem((2, 2, 2, 3, 48, 256), BF16), vmem((64, 128), jnp.int32), vmem((2, 84, 512), F32),
            vmem((2, 96, 256), F32),
            dma((4, 4)), dma((4, 2)), dma((4, 2)), dma((4,)), dma((4,)), dma((4,)), dma((4,)), dma((4, 2)), dma((4, 2)), dma((4, 3)), dma((4, 3)),
            dma((4,)), dma((4,)), dma((2, 2)), dma((2, 4)), dma((2, 3, 2)), dma((2, 8)), dma((2, 8)),
            dma((2, 2, 2, 4)), dma((2, 2, 2, 4)), dma((2, 2, 2, 3)), dma((2, 2, 2, 3)), dma(()), dma((2,)), dma((2, 4)), dma((2, 4)),
            dma((2, 2)), dma((4,)), dma((4,)), dma((4,)), dma((4,)),
        ],
        compiler_params=pltpu.CompilerParams(
            collective_id=0, has_side_effects=True, vmem_limit_bytes=60 << 20),
        cost_estimate=pl.CostEstimate(flops=3_000_000_000, bytes_accessed=12_000_000, transcendentals=1_200_000),
    )(x, queries, keys, values, grad_out, docs)
    return tuple(pl.pallas_call(
        copies,
        name="results",
        out_shape=outs,
        in_specs=[anywhere] * 5,
        out_specs=(anywhere,) * 5,
        scratch_shapes=[vmem(o.shape, o.dtype) for o in outs] + [dma((2, 5))],
        compiler_params=pltpu.CompilerParams(vmem_limit_bytes=60 << 20),
    )(*results))


def solution(mesh):
    return jax.shard_map(
        local,
        mesh=mesh,
        in_specs=(P(None, "seq"), P("seq", "head"), P("seq", "head"), P("seq", "head"), P("seq", "head"), P()),
        out_specs=(P("seq", "head"),) * 5,
        check_vma=False,
    )
```

```python
import jax
import jax.numpy as jnp
from jax import lax
from jax.experimental import pallas as pl
from jax.experimental.pallas import tpu as pltpu
from jax.sharding import PartitionSpec as P

MESH = pl.DeviceIdType.MESH
SCALE = 168.0 ** -0.5
LOG2E = 1.4426950408889634
NEG = -1.0e30
T = 128
HALF = 512
WIN = 1536
SPAN = 1152
NZ = 8
F32 = jnp.float32
BF16 = jnp.bfloat16


def dims(lhs, rhs, lc, rc):
    return lax.dot_general(lhs, rhs, (((lc,), (rc,)), ((), ())), preferred_element_type=F32)


def kernel(
    x_ref, q_ref, k_ref, v_ref, o_ref, doc_hbm,
    dq_out, dk_out, dv_out, wk_out, wv_out,
    qb, ob, kv, xb, acck, accv, lo_ref, dqs, t1s, tr1, t2s, tr2, gs, gb, pbuf, sdn, sup, rdn, rup, doc_ref, fin, precv, sbuf, gbuf,
    a_send, a_kv, a_q, z_send, z_recv, s_send, s_recv, x_send, x_recv, xs_send, xs_recv,
    dq_send, dq_recv, t1_sem, t2_sem, d_send, d_recv, f_send, dn_send, dn_recv, up_send, up_recv, doc_sem, out_sem, g_send, g_recv, p_sem,
    xf_send, xf_recv, xg_send, xg_recv,
):
    seq = lax.axis_index("seq")
    head = lax.axis_index("head")
    z = seq // 8
    i = seq % 8
    xl = head // 2
    core = head % 2
    own_half = i // 4
    lane = i % 4
    self_a = core == own_half
    y = i // 2
    xh = i % 2

    def dev(zz, ii, cc):
        return (zz * 8 + ii, xl * 2 + cc)

    up = lax.rem(z + 1, NZ)
    down = lax.rem(z + NZ - 1, NZ)
    sibling = dev(z, i, 1 - core)
    above = dev(up, i, core)
    below = dev(down, i, core)

    def remote(src, dst, ssem, rsem, device):
        return pltpu.make_async_remote_copy(
            src_ref=src, dst_ref=dst, send_sem=ssem, recv_sem=rsem, device_id=device, device_id_type=MESH)

    def got(dst, sem):
        pltpu.make_async_copy(dst, dst, sem).wait()

    docs = pltpu.make_async_copy(doc_hbm, doc_ref, doc_sem)
    docs.start()
    barrier = pltpu.get_barrier_semaphore()

    @pl.loop(1, 8)
    def _(step):
        for cc in range(2):
            pl.semaphore_signal(barrier, inc=1, device_id=dev(z, lax.rem(i + step, 8), cc), device_id_type=MESH)

    across = dev(jnp.where(core == 0, down, up), i, 1 - core)
    flip = i + 1 - 2 * xh

    def opposite(yy):
        return (z * 8 + yy * 2 + 1 - xh, (1 - xl) * 2 + core)

    beside = (seq, (1 - xl) * 2 + core)
    for other in (sibling, above, below, across, beside, dev(up, flip, core), dev(down, flip, core)):
        pl.semaphore_signal(barrier, inc=1, device_id=other, device_id_type=MESH)

    @pl.loop(0, 4)
    def _(yy):
        pl.semaphore_signal(barrier, inc=1, device_id=opposite(yy), device_id_type=MESH)

    pl.semaphore_wait(barrier, 25)

    def a_parts(l):
        row = pl.multiple_of(lane * T, T)
        c1 = pl.multiple_of(l * T, T)
        c2 = pl.multiple_of(l * 2 * T, 2 * T)
        return (
            (k_ref.at[:, pl.ds(c1, T)], kv.at[pl.ds(1024 + row, T), pl.ds(0, T)], a_send.at[l, 0], a_kv.at[lane, 0]),
            (v_ref.at[:, pl.ds(c1, T)], kv.at[pl.ds(1024 + row, T), pl.ds(T, T)], a_send.at[l, 1], a_kv.at[lane, 1]),
            (q_ref.at[:, pl.ds(c2, 2 * T)], qb.at[pl.ds(row, T)], a_send.at[l, 2], a_q.at[lane, 0]),
            (o_ref.at[:, pl.ds(c2, 2 * T)], ob.at[pl.ds(row, T)], a_send.at[l, 3], a_q.at[lane, 1]),
        )

    def a_start(first, last):
        @pl.loop(0, 4)
        def _(step):
            l = lax.rem(lane + step, 4)
            mine = self_a & (l == lane)

            @pl.when(mine)
            def _():
                for src, dst, ssem, rsem in a_parts(l)[first:last]:
                    pltpu.make_async_copy(src, dst, rsem).start()

            @pl.when(jnp.logical_not(mine))
            def _():
                for src, dst, ssem, rsem in a_parts(l)[first:last]:
                    remote(src, dst, ssem, rsem, dev(z, 4 * core + l, own_half)).start()

    a_start(0, 2)
    a_start(2, 4)

    zs = pl.ds(4 * core, 4)
    others = pl.ds(4 * (1 - core), 4)

    def x_part(yy, sub):
        row = 2 * yy + sub
        start = pl.multiple_of(84 * row - 4 * (row % 4), 16)
        return x_ref.at[zs, pl.ds(start, 96), :], xb.at[sub, i, zs]

    def x_copy(step, sub):
        yy = lax.rem(y + step, 4)
        src, dst = x_part(yy, sub)
        return remote(src, dst, x_send.at[step, sub], x_recv.at[y, sub], dev(z, yy * 2 + xh, core))

    def x_across(step):
        yy = lax.rem(y + step, 4)
        src, dst = x_part(yy, xl)
        return remote(src, dst, xf_send.at[step], xf_recv.at[y], opposite(yy))

    def x_beside(ys):
        piece = xb.at[1 - xl, ys * 2 + 1 - xh, zs]
        return remote(piece, piece, xg_send.at[ys], xg_recv.at[ys], beside)

    def xs_own(ys):
        piece = xb.at[:, ys * 2 + xh, zs]
        return remote(piece, piece, xs_send.at[ys, 0], xs_recv.at[ys, 0], sibling)

    def xs_other(ys, s):
        piece = xb.at[1 - xl if s == 0 else xl, ys * 2 + 1 - xh, zs]
        return remote(piece, piece, xs_send.at[ys, 1 + s], xs_recv.at[ys, 1 + s], sibling)

    def near_first(b):
        return lax.rem(y + jnp.where(b < 2, b, 5 - b), 4)

    def x_start():
        for sub in range(2):
            src, dst = x_part(y, sub)
            pltpu.make_async_copy(src, dst, x_recv.at[y, sub]).start()

        @pl.loop(0, 4)
        def _(b):
            x_across(jnp.where(b < 2, b, 5 - b)).start()

        @pl.loop(1, 4)
        def _(b):
            for sub in range(2):
                x_copy(jnp.where(b < 2, b, 5 - b), sub).start()

    def x_arrived(ys):
        for sub in range(2):
            got(xb.at[sub, ys * 2 + xh, zs], x_recv.at[ys, sub])
        xs_own(ys).start()

    def x_second(b):
        ys = near_first(b)
        got(xb.at[1 - xl, ys * 2 + 1 - xh, zs], xf_recv.at[ys])
        x_beside(ys).start()
        xs_other(ys, 0).start()

    def x_third(b):
        ys = near_first(b)
        got(xb.at[xl, ys * 2 + 1 - xh, zs], xg_recv.at[ys])
        xs_other(ys, 1).start()

    def x_complete():
        @pl.loop(0, 4)
        def _(ys):
            got(xb.at[:, ys * 2 + xh, others], xs_recv.at[ys, 0])
            got(xb.at[1 - xl, ys * 2 + 1 - xh, others], xs_recv.at[ys, 1])
            got(xb.at[xl, ys * 2 + 1 - xh, others], xs_recv.at[ys, 2])

    docs.wait()
    ids = doc_ref[pl.ds((2 * z + core) * 4, 4), :]
    table = doc_ref[...]
    begin = jnp.zeros((4, T), F32)
    for d in range(15):
        count = jnp.sum(jnp.where(table == d, 1.0, 0.0), axis=(0, 1), keepdims=True)
        begin = begin + jnp.where(ids > d, 1.0, 0.0) * count
    begin = begin.astype(jnp.int32) - (2 * z + core - 2) * HALF
    place = lax.broadcasted_iota(jnp.int32, (4, T), 1) + lax.broadcasted_iota(jnp.int32, (4, T), 0) * T
    lo_ref[0:4, :] = jnp.maximum(begin, place + 1)

    acck[...] = jnp.zeros_like(acck)
    accv[...] = jnp.zeros_like(accv)

    def rows(base, m):
        return pl.ds(pl.multiple_of(base + m * T, T), T)

    def z_copy(m):
        return remote(kv.at[rows(1024, m)], kv.at[rows(0, m)], z_send.at[m], z_recv.at[m], above)

    def s_copy(m):
        base = jnp.where(core == 0, 1024, 0)
        return remote(kv.at[rows(base, m)], kv.at[rows(512, m)], s_send.at[m], s_recv.at[m], sibling)

    @pl.loop(0, 4)
    def _(m):
        got(kv.at[rows(1024, m), pl.ds(0, T)], a_kv.at[m, 0])
        got(kv.at[rows(1024, m), pl.ds(T, T)], a_kv.at[m, 1])
        z_copy(m).start()

        @pl.when(core == 0)
        def _():
            s_copy(m).start()

    x_start()

    @pl.loop(0, 4)
    def _(m):
        z_copy(m).wait_recv()

        @pl.when(core == 1)
        def _():
            s_copy(m).start()

    @pl.loop(0, 4)
    def _(m):
        s_copy(m).wait_recv()
        got(qb.at[rows(0, m)], a_q.at[m, 0])
        got(ob.at[rows(0, m)], a_q.at[m, 1])

    def t2_copy(b):
        return remote(t2s.at[rows(0, b)], tr2.at[rows(0, b)], t2_sem.at[0, b], t2_sem.at[1, b], below)

    def dq_copy(m):
        col = pl.ds(pl.multiple_of(lane * 2 * T, 2 * T), 2 * T)
        return dqs.at[rows(0, m)], dq_out.at[:, col], dq_send.at[m], dq_recv.at[lane], dev(z, 4 * core + m, own_half)

    def pair(ref, b):
        return jnp.concatenate([ref[b * T:(b + 1) * T, 0:T], ref[b * T:(b + 1) * T, T:2 * T]], 0)

    def first_products(b):
        sbuf[b % 2] = dims(kv[b * T:b * T + SPAN, 0:T], pair(qb, b), 1, 1)
        gbuf[b % 2] = dims(kv[b * T:b * T + SPAN, T:2 * T], pair(ob, b), 1, 1)

    spot = lax.broadcasted_iota(jnp.int32, (1024, 2 * T), 0)
    tail = lax.broadcasted_iota(jnp.int32, (T, 2 * T), 0) + 1024
    high = 1024 + lax.broadcasted_iota(jnp.int32, (1, 2 * T), 1) % T
    first_products(0)
    for b in range(4):
        here = slice(b * T, (b + 1) * T)
        span = slice(b * T, b * T + SPAN)
        if b == 1:
            x_second(0)
        if b < 3:
            first_products(b + 1)
        low = lo_ref[b:b + 1, :] - b * T
        low = jnp.concatenate([low, low], 1)
        scores = jnp.concatenate([
            jnp.where(spot >= low, sbuf[b % 2, 0:1024], NEG),
            jnp.where((tail >= low) & (tail <= high), sbuf[b % 2, 1024:SPAN], NEG)], 0)
        top = jnp.max(scores, axis=0, keepdims=True)
        expo = jnp.exp2((scores - top) * (SCALE * LOG2E))
        probs = expo * (1.0 / jnp.sum(expo, axis=0, keepdims=True))
        grad_probs = gbuf[b % 2]
        delta = jnp.sum(probs * grad_probs, axis=0, keepdims=True)
        grad_scores = (SCALE * probs * (grad_probs - delta)).astype(BF16)
        accv[span, :] += dims(probs.astype(BF16), pair(ob, b), 1, 0)
        acck[span, :] += dims(grad_scores, pair(qb, b), 1, 0)
        t2s[here, 0:T] = acck[here, :].astype(BF16)
        t2s[here, T:2 * T] = accv[here, :].astype(BF16)
        t2_copy(b).start()
        dq2 = dims(grad_scores, kv[span, 0:T], 0, 0).astype(BF16)
        dqs[here, 0:T] = dq2[:T]
        dqs[here, T:2 * T] = dq2[T:]
        mine = self_a & (b == lane)
        src, dst, ssem, rsem, to = dq_copy(b)

        @pl.when(mine)
        def _():
            pltpu.make_async_copy(src, dst, rsem).start()

        @pl.when(jnp.logical_not(mine))
        def _():
            remote(src, dst, ssem, rsem, to).start()

    owner = dev(jnp.where(core == 0, down, z), i, 1 - core)

    def t1_copy(part):
        return remote(t1s.at[part], tr1.at[part], t1_sem.at[0, part], t1_sem.at[1, part], owner)

    for part, total in enumerate((accv, acck)):
        t1s[part] = total[512:1024, :].astype(BF16)
        t1_copy(part).start()

    @pl.loop(1, 4)
    def _(b):
        x_second(b)

    @pl.loop(0, 4)
    def _(b):
        x_arrived(near_first(b))

    @pl.loop(0, 4)
    def _(b):
        t2_copy(b).wait_recv()

    right = lax.rem(y + 1, 4) * 2 + xh
    left = lax.rem(y + 3, 4) * 2 + xh

    def block(part, u, a, h):
        return gb.at[part, pl.ds(pl.multiple_of(a * HALF + h * 256, 256), 256), pl.ds(pl.multiple_of(u * T, T), T)]

    def d_copy(part, n, h):
        to = dev(z, (right, left, i)[n], own_half)
        return (gs.at[part, pl.ds(h * 256, 256)], block(part, y % 2, core, h), d_send.at[part, n, h],
                d_recv.at[part, (y % 2) * 4 + core * 2 + h], to)

    def forward(part, u, a, h):
        piece = block(part, u, a, h)
        n = u * 4 + a * 2 + h
        return remote(piece, piece, f_send.at[part, n], d_recv.at[part, n], dev(z, jnp.where(h == 0, right, left), core))

    def arrived(part, u, a, h):
        got(block(part, u, a, h), d_recv.at[part, u * 4 + a * 2 + h])

    def steps_from(u):
        return lax.rem(y - 2 * core - u + 8, 4)

    def first_send(part):
        for h in range(2):
            for n in range(2):
                src, dst, ssem, rsem, to = d_copy(part, n, (h + n) % 2)
                remote(src, dst, ssem, rsem, to).start()
        for h in range(2):
            src, dst, ssem, rsem, to = d_copy(part, 2, h)

            @pl.when(self_a)
            def _():
                pltpu.make_async_copy(src, dst, rsem).start()

            @pl.when(jnp.logical_not(self_a))
            def _():
                remote(src, dst, ssem, rsem, to).start()

    def forward_side(part):
        @pl.loop(0, 4)
        def _(e):
            u, a = e // 2, e % 2
            steps = steps_from(u)

            @pl.when((steps == 1) | (steps == 3))
            def _():
                h = jnp.where(steps == 1, 0, 1)
                arrived(part, u, a, h)
                forward(part, u, a, h).start()

    def gathered(part):
        @pl.loop(0, 4)
        def _(e):
            u, a = e // 2, e % 2
            steps = steps_from(u)

            @pl.when((steps == 2) | (steps == 0))
            def _():
                arrived(part, u, a, 0)
                arrived(part, u, a, 1)

            @pl.when((steps == 1) | (steps == 3))
            def _():
                arrived(part, u, a, jnp.where(steps == 1, 1, 0))

    def sent(part):
        for n in range(2):
            for h in range(2):
                src, dst, ssem, rsem, to = d_copy(part, n, h)
                remote(src, dst, ssem, rsem, to).wait_send()

        @pl.when(jnp.logical_not(self_a))
        def _():
            for h in range(2):
                src, dst, ssem, rsem, to = d_copy(part, 2, h)
                remote(src, dst, ssem, rsem, to).wait_send()

        @pl.loop(0, 4)
        def _(e):
            u, a = e // 2, e % 2
            steps = steps_from(u)

            @pl.when((steps == 1) | (steps == 3))
            def _():
                forward(part, u, a, jnp.where(steps == 1, 0, 1)).wait_send()

    def g_copy(part, m):
        col = pl.ds(pl.multiple_of(lane * T, T), T)
        return (gs.at[part, rows(0, m)], (dv_out, dk_out)[part].at[:, col], g_send.at[part, m], g_recv.at[part, lane],
                dev(z, 4 * core + m, own_half))

    def token_send(part):
        @pl.loop(0, 4)
        def _(m):
            mine = self_a & (m == lane)
            src, dst, ssem, rsem, to = g_copy(part, m)

            @pl.when(mine)
            def _():
                pltpu.make_async_copy(src, dst, rsem).start()

            @pl.when(jnp.logical_not(mine))
            def _():
                remote(src, dst, ssem, rsem, to).start()

    def token_wait(part):
        @pl.loop(0, 4)
        def _(m):
            got((dv_out, dk_out)[part].at[:, pl.ds(pl.multiple_of(m * T, T), T)], g_recv.at[part, m])
            src, dst, ssem, rsem, to = g_copy(part, m)

            @pl.when(jnp.logical_not(self_a & (m == lane)))
            def _():
                remote(src, dst, ssem, rsem, to).wait_send()

    for part, total in enumerate((accv, acck)):
        t1_copy(part).wait_recv()
        cols = pl.ds((1 - part) * T, T)
        gs[part] = (total[1024:1536, :] + tr1[part].astype(F32) + tr2[:, cols].astype(F32)).astype(BF16)
        first_send(part)


    def dest(offset):
        return lax.rem(z + offset + NZ, NZ)

    def long_copy(part, sub, h, k):
        slot, ii = (xh, (i // 2) * 2 + sub) if k == 3 else (sub, i)
        return remote(sdn.at[part, sub, h, k], rdn.at[part, slot, h, k], dn_send.at[part, sub, h, k],
                      dn_recv.at[part, slot, h, k], dev(down if sub == 0 else up, ii, core))

    def short_copy(part, sub, h, k):
        slot, ii = (xh, (i // 2) * 2 + sub) if k == 2 else (sub, i)
        return remote(sup.at[part, sub, h, k], rup.at[part, slot, h, k], up_send.at[part, sub, h, k],
                      up_recv.at[part, slot, h, k], dev(up if sub == 0 else down, ii, core))

    def ring(part, k):
        for h in range(2):
            lines = slice(h * 48, h * 48 + 48)
            for sub in range(2):
                way = -1 if sub == 0 else 1
                value = pbuf[part, sub, dest(way * (4 - k)), lines]
                if k > 0:
                    got(rdn.at[part, sub, h, k - 1], dn_recv.at[part, sub, h, k - 1])
                    value = value + rdn[part, sub, h, k - 1].astype(F32)
                sdn[part, sub, h, k] = value.astype(BF16)
                long_copy(part, sub, h, k).start()
            if k < 3:
                for sub in range(2):
                    way = -1 if sub == 0 else 1
                    value = pbuf[part, sub, dest(-way * (3 - k)), lines]
                    if k > 0:
                        got(rup.at[part, sub, h, k - 1], up_recv.at[part, sub, h, k - 1])
                        value = value + rup[part, sub, h, k - 1].astype(F32)
                    sup[part, sub, h, k] = value.astype(BF16)
                    short_copy(part, sub, h, k).start()

    def product(part):
        @pl.loop(0, 4)
        def _(n):
            at = pl.ds((n % 2) * 4, 4)
            lhs = jnp.concatenate([xb[n // 2, j, at].reshape(384, T) for j in range(8)], 1)
            pbuf[part, n // 2, at] = jnp.dot(lhs, gb[part], preferred_element_type=F32).reshape(4, 96, 256)

    def p_copy(part):
        return remote(pbuf.at[part, 1 - xh, z], precv.at[part], p_sem.at[0, part], p_sem.at[1, part], dev(z, flip, core))

    offset = 4 * (i % 4)

    def weight_copy(part):
        return pltpu.make_async_copy(fin.at[part], (wv_out, wk_out)[part], out_sem.at[part])

    def finish(part):
        p_copy(part).wait_recv()
        for s in range(2):
            pieces = []
            for h in range(2):
                got(rdn.at[part, s, h, 3], dn_recv.at[part, s, h, 3])
                got(rup.at[part, s, h, 2], up_recv.at[part, s, h, 2])
                pieces.append(rdn[part, s, h, 3].astype(F32) + rup[part, s, h, 2].astype(F32))
            total = jnp.concatenate(pieces, 0) + jnp.where(xh == s, pbuf[part, s, z], precv[part])
            total = pltpu.roll(total, lax.rem(96 - offset, 96), 0)
            for u in range(2):
                fin[part, :, (u * 2 + s) * T:(u * 2 + s + 1) * T] = total[:84, u * T:(u + 1) * T]
        weight_copy(part).start()

    forward_side(0)
    forward_side(1)
    token_send(0)
    token_send(1)

    @pl.loop(0, 4)
    def _(b):
        x_third(b)

    gathered(0)
    x_complete()
    product(0)
    ring(0, 0)
    p_copy(0).start()
    ring(0, 1)
    gathered(1)
    product(1)
    ring(1, 0)
    p_copy(1).start()
    ring(0, 2)
    ring(1, 1)
    ring(0, 3)
    ring(1, 2)
    ring(1, 3)
    finish(0)
    finish(1)
    token_wait(0)
    token_wait(1)

    @pl.loop(0, 4)
    def _(l):
        got(dq_out.at[:, pl.ds(pl.multiple_of(l * 2 * T, 2 * T), 2 * T)], dq_recv.at[l])

    @pl.loop(0, 4)
    def _(m):
        z_copy(m).wait_send()
        s_copy(m).wait_send()
        src, dst, ssem, rsem, to = dq_copy(m)

        @pl.when(jnp.logical_not(self_a & (m == lane)))
        def _():
            for src_a, dst_a, ssem_a, rsem_a in a_parts(m):
                remote(src_a, dst_a, ssem_a, rsem_a, dev(z, 4 * core + m, own_half)).wait_send()
            remote(src, dst, ssem, rsem, to).wait_send()

    @pl.loop(0, 4)
    def _(b):
        t2_copy(b).wait_send()


    @pl.loop(0, 4)
    def _(ys):
        x_across(ys).wait_send()
        x_beside(ys).wait_send()
        xs_own(ys).wait_send()
        for s in range(2):
            xs_other(ys, s).wait_send()

    @pl.loop(1, 4)
    def _(step):
        for sub in range(2):
            x_copy(step, sub).wait_send()

    for part in range(2):
        t1_copy(part).wait_send()
        sent(part)
        weight_copy(part).wait()
        p_copy(part).wait_send()
        for sub in range(2):
            for h in range(2):
                for k in range(4):
                    long_copy(part, sub, h, k).wait_send()
                for k in range(3):
                    short_copy(part, sub, h, k).wait_send()


def copies(*refs):
    count = 5
    inputs, outputs, held, sem = refs[:count], refs[count:2 * count], refs[2 * count:3 * count], refs[-1]
    loads = [pltpu.make_async_copy(inputs[n], held[n], sem.at[0, n]) for n in range(count)]
    stores = [pltpu.make_async_copy(held[n], outputs[n], sem.at[1, n]) for n in range(count)]
    for load in loads:
        load.start()
    for load, store in zip(loads, stores):
        load.wait()
        store.start()
    for store in stores:
        store.wait()


def local(inputs, queries, keys, values, grad_out, doc_ids):
    x = inputs.reshape(8, 672, 128)
    docs = doc_ids.reshape(64, 128)
    anywhere = pl.BlockSpec(memory_space=pl.ANY)
    dma = pltpu.SemaphoreType.DMA
    shape = jax.ShapeDtypeStruct
    vmem = pltpu.VMEM
    outs = (
        shape((T, 1024), BF16), shape((T, 512), BF16), shape((T, 512), BF16), shape((84, 512), F32), shape((84, 512), F32))
    results = pl.pallas_call(
        kernel,
        name="window_backward",
        out_shape=outs,
        in_specs=[anywhere] * 6,
        out_specs=(anywhere,) * 5,
        scratch_shapes=[
            vmem((512, 256), BF16), vmem((512, 256), BF16), vmem((WIN, 256), BF16),
            vmem((2, 8, 8, 96, T), BF16), vmem((WIN, T), F32), vmem((WIN, T), F32),
            vmem((8, T), jnp.int32), vmem((512, 256), BF16),
            vmem((2, 512, T), BF16), vmem((2, 512, T), BF16), vmem((512, 256), BF16), vmem((512, 256), BF16),
            vmem((2, 512, T), BF16), vmem((2, 1024, 256), BF16),
            vmem((2, 2, 8, 96, 256), F32),
            vmem((2, 2, 2, 4, 48, 256), BF16), vmem((2, 2, 2, 3, 48, 256), BF16),
            vmem((2, 2, 2, 4, 48, 256), BF16), vmem((2, 2, 2, 3, 48, 256), BF16), vmem((64, 128), jnp.int32), vmem((2, 84, 512), F32),
            vmem((2, 96, 256), F32), vmem((2, SPAN, 256), F32), vmem((2, SPAN, 256), F32),
            dma((4, 4)), dma((4, 2)), dma((4, 2)), dma((4,)), dma((4,)), dma((4,)), dma((4,)), dma((4, 2)), dma((4, 2)), dma((4, 3)), dma((4, 3)),
            dma((4,)), dma((4,)), dma((2, 2)), dma((2, 4)), dma((2, 3, 2)), dma((2, 8)), dma((2, 8)),
            dma((2, 2, 2, 4)), dma((2, 2, 2, 4)), dma((2, 2, 2, 3)), dma((2, 2, 2, 3)), dma(()), dma((2,)), dma((2, 4)), dma((2, 4)),
            dma((2, 2)), dma((4,)), dma((4,)), dma((4,)), dma((4,)),
        ],
        compiler_params=pltpu.CompilerParams(
            collective_id=0, has_side_effects=True, vmem_limit_bytes=60 << 20),
        cost_estimate=pl.CostEstimate(flops=3_000_000_000, bytes_accessed=12_000_000, transcendentals=1_200_000),
    )(x, queries, keys, values, grad_out, docs)
    return tuple(pl.pallas_call(
        copies,
        name="results",
        out_shape=outs,
        in_specs=[anywhere] * 5,
        out_specs=(anywhere,) * 5,
        scratch_shapes=[vmem(o.shape, o.dtype) for o in outs] + [dma((2, 5))],
        compiler_params=pltpu.CompilerParams(vmem_limit_bytes=60 << 20),
    )(*results))


def solution(mesh):
    return jax.shard_map(
        local,
        mesh=mesh,
        in_specs=(P(None, "seq"), P("seq", "head"), P("seq", "head"), P("seq", "head"), P("seq", "head"), P()),
        out_specs=(P("seq", "head"),) * 5,
        check_vma=False,
    )
```

```python
import jax
import jax.numpy as jnp
from jax import lax
from jax.experimental import pallas as pl
from jax.experimental.pallas import tpu as pltpu
from jax.sharding import PartitionSpec as P

MESH = pl.DeviceIdType.MESH
SCALE = 168.0 ** -0.5
LOG2E = 1.4426950408889634
NEG = -1.0e30
T = 128
HALF = 512
WIN = 1536
SPAN = 1152
NZ = 8
F32 = jnp.float32
BF16 = jnp.bfloat16


def dims(lhs, rhs, lc, rc):
    return lax.dot_general(lhs, rhs, (((lc,), (rc,)), ((), ())), preferred_element_type=F32)


def kernel(
    x_ref, q_ref, k_ref, v_ref, o_ref, doc_hbm,
    dq_out, dk_out, dv_out, wk_out, wv_out,
    qb, ob, kv, xb, acck, accv, lo_ref, dqs, t1s, tr1, t2s, tr2, gs, gb, pbuf, sdn, sup, rdn, rup, doc_ref, fin, precv, sbuf, gbuf,
    a_send, a_kv, a_q, z_send, z_recv, s_send, s_recv, x_send, x_recv, xs_send, xs_recv,
    dq_send, dq_recv, t1_sem, t2_sem, d_send, d_recv, f_send, dn_send, dn_recv, up_send, up_recv, doc_sem, out_sem, g_send, g_recv, p_sem,
    xf_send, xf_recv, xg_send, xg_recv,
):
    seq = lax.axis_index("seq")
    head = lax.axis_index("head")
    z = seq // 8
    i = seq % 8
    xl = head // 2
    core = head % 2
    own_half = i // 4
    lane = i % 4
    self_a = core == own_half
    y = i // 2
    xh = i % 2

    def dev(zz, ii, cc):
        return (zz * 8 + ii, xl * 2 + cc)

    up = lax.rem(z + 1, NZ)
    down = lax.rem(z + NZ - 1, NZ)
    sibling = dev(z, i, 1 - core)
    above = dev(up, i, core)
    below = dev(down, i, core)

    def remote(src, dst, ssem, rsem, device):
        return pltpu.make_async_remote_copy(
            src_ref=src, dst_ref=dst, send_sem=ssem, recv_sem=rsem, device_id=device, device_id_type=MESH)

    def got(dst, sem):
        pltpu.make_async_copy(dst, dst, sem).wait()

    docs = pltpu.make_async_copy(doc_hbm, doc_ref, doc_sem)
    docs.start()
    barrier = pltpu.get_barrier_semaphore()

    @pl.loop(1, 8)
    def _(step):
        for cc in range(2):
            pl.semaphore_signal(barrier, inc=1, device_id=dev(z, lax.rem(i + step, 8), cc), device_id_type=MESH)

    across = dev(jnp.where(core == 0, down, up), i, 1 - core)
    flip = i + 1 - 2 * xh

    def opposite(yy):
        return (z * 8 + yy * 2 + 1 - xh, (1 - xl) * 2 + core)

    beside = (seq, (1 - xl) * 2 + core)
    for other in (sibling, above, below, across, beside, dev(up, flip, core), dev(down, flip, core)):
        pl.semaphore_signal(barrier, inc=1, device_id=other, device_id_type=MESH)

    @pl.loop(0, 4)
    def _(yy):
        pl.semaphore_signal(barrier, inc=1, device_id=opposite(yy), device_id_type=MESH)

    pl.semaphore_wait(barrier, 25)

    def a_parts(l):
        row = pl.multiple_of(lane * T, T)
        c1 = pl.multiple_of(l * T, T)
        c2 = pl.multiple_of(l * 2 * T, 2 * T)
        return (
            (k_ref.at[:, pl.ds(c1, T)], kv.at[pl.ds(1024 + row, T), pl.ds(0, T)], a_send.at[l, 0], a_kv.at[lane, 0]),
            (v_ref.at[:, pl.ds(c1, T)], kv.at[pl.ds(1024 + row, T), pl.ds(T, T)], a_send.at[l, 1], a_kv.at[lane, 1]),
            (q_ref.at[:, pl.ds(c2, 2 * T)], qb.at[pl.ds(row, T)], a_send.at[l, 2], a_q.at[lane, 0]),
            (o_ref.at[:, pl.ds(c2, 2 * T)], ob.at[pl.ds(row, T)], a_send.at[l, 3], a_q.at[lane, 1]),
        )

    def a_start(first, last):
        @pl.loop(0, 4)
        def _(step):
            l = lax.rem(lane + step, 4)
            mine = self_a & (l == lane)

            @pl.when(mine)
            def _():
                for src, dst, ssem, rsem in a_parts(l)[first:last]:
                    pltpu.make_async_copy(src, dst, rsem).start()

            @pl.when(jnp.logical_not(mine))
            def _():
                for src, dst, ssem, rsem in a_parts(l)[first:last]:
                    remote(src, dst, ssem, rsem, dev(z, 4 * core + l, own_half)).start()

    a_start(0, 2)
    a_start(2, 4)

    zs = pl.ds(4 * core, 4)
    others = pl.ds(4 * (1 - core), 4)

    def x_part(yy, sub):
        row = 2 * yy + sub
        start = pl.multiple_of(84 * row - 4 * (row % 4), 16)
        return x_ref.at[zs, pl.ds(start, 96), :], xb.at[sub, i, zs]

    def x_copy(step, sub):
        yy = lax.rem(y + step, 4)
        src, dst = x_part(yy, sub)
        return remote(src, dst, x_send.at[step, sub], x_recv.at[y, sub], dev(z, yy * 2 + xh, core))

    def x_across(step):
        yy = lax.rem(y + step, 4)
        src, dst = x_part(yy, xl)
        return remote(src, dst, xf_send.at[step], xf_recv.at[y], opposite(yy))

    def x_beside(ys):
        piece = xb.at[1 - xl, ys * 2 + 1 - xh, zs]
        return remote(piece, piece, xg_send.at[ys], xg_recv.at[ys], beside)

    def xs_own(ys):
        piece = xb.at[:, ys * 2 + xh, zs]
        return remote(piece, piece, xs_send.at[ys, 0], xs_recv.at[ys, 0], sibling)

    def xs_other(ys, s):
        piece = xb.at[1 - xl if s == 0 else xl, ys * 2 + 1 - xh, zs]
        return remote(piece, piece, xs_send.at[ys, 1 + s], xs_recv.at[ys, 1 + s], sibling)

    def near_first(b):
        return lax.rem(y + jnp.where(b < 2, b, 5 - b), 4)

    def x_start():
        for sub in range(2):
            src, dst = x_part(y, sub)
            pltpu.make_async_copy(src, dst, x_recv.at[y, sub]).start()

        @pl.loop(0, 4)
        def _(b):
            x_across(jnp.where(b < 2, b, 5 - b)).start()

        @pl.loop(1, 4)
        def _(b):
            for sub in range(2):
                x_copy(jnp.where(b < 2, b, 5 - b), sub).start()

    def x_arrived(ys):
        for sub in range(2):
            got(xb.at[sub, ys * 2 + xh, zs], x_recv.at[ys, sub])
        xs_own(ys).start()

    def x_second(b):
        ys = near_first(b)
        got(xb.at[1 - xl, ys * 2 + 1 - xh, zs], xf_recv.at[ys])
        x_beside(ys).start()
        xs_other(ys, 0).start()

    def x_third(b):
        ys = near_first(b)
        got(xb.at[xl, ys * 2 + 1 - xh, zs], xg_recv.at[ys])
        xs_other(ys, 1).start()

    def x_complete():
        @pl.loop(0, 4)
        def _(ys):
            got(xb.at[:, ys * 2 + xh, others], xs_recv.at[ys, 0])
            got(xb.at[1 - xl, ys * 2 + 1 - xh, others], xs_recv.at[ys, 1])
            got(xb.at[xl, ys * 2 + 1 - xh, others], xs_recv.at[ys, 2])

    docs.wait()
    ids = doc_ref[pl.ds((2 * z + core) * 4, 4), :]
    table = doc_ref[...]
    begin = jnp.zeros((4, T), F32)
    for d in range(15):
        count = jnp.sum(jnp.where(table == d, 1.0, 0.0), axis=(0, 1), keepdims=True)
        begin = begin + jnp.where(ids > d, 1.0, 0.0) * count
    begin = begin.astype(jnp.int32) - (2 * z + core - 2) * HALF
    place = lax.broadcasted_iota(jnp.int32, (4, T), 1) + lax.broadcasted_iota(jnp.int32, (4, T), 0) * T
    lo_ref[0:4, :] = jnp.maximum(begin, place + 1)

    acck[...] = jnp.zeros_like(acck)
    accv[...] = jnp.zeros_like(accv)

    def rows(base, m):
        return pl.ds(pl.multiple_of(base + m * T, T), T)

    def z_copy(m):
        return remote(kv.at[rows(1024, m)], kv.at[rows(0, m)], z_send.at[m], z_recv.at[m], above)

    def s_copy(m):
        base = jnp.where(core == 0, 1024, 0)
        return remote(kv.at[rows(base, m)], kv.at[rows(512, m)], s_send.at[m], s_recv.at[m], sibling)

    @pl.loop(0, 4)
    def _(m):
        got(kv.at[rows(1024, m), pl.ds(0, T)], a_kv.at[m, 0])
        got(kv.at[rows(1024, m), pl.ds(T, T)], a_kv.at[m, 1])
        z_copy(m).start()

        @pl.when(core == 0)
        def _():
            s_copy(m).start()

    x_start()

    @pl.loop(0, 4)
    def _(m):
        z_copy(m).wait_recv()

        @pl.when(core == 1)
        def _():
            s_copy(m).start()

    @pl.loop(0, 4)
    def _(m):
        s_copy(m).wait_recv()
        got(qb.at[rows(0, m)], a_q.at[m, 0])
        got(ob.at[rows(0, m)], a_q.at[m, 1])

    def t2_copy(b):
        return remote(t2s.at[rows(0, b)], tr2.at[rows(0, b)], t2_sem.at[0, b], t2_sem.at[1, b], below)

    def dq_copy(m):
        col = pl.ds(pl.multiple_of(lane * 2 * T, 2 * T), 2 * T)
        return dqs.at[rows(0, m)], dq_out.at[:, col], dq_send.at[m], dq_recv.at[lane], dev(z, 4 * core + m, own_half)

    def pair(ref, b):
        return jnp.concatenate([ref[b * T:(b + 1) * T, 0:T], ref[b * T:(b + 1) * T, T:2 * T]], 0)

    def first_products(b):
        sbuf[b % 2] = dims(kv[b * T:b * T + SPAN, 0:T], pair(qb, b), 1, 1)
        gbuf[b % 2] = dims(kv[b * T:b * T + SPAN, T:2 * T], pair(ob, b), 1, 1)

    spot = lax.broadcasted_iota(jnp.int32, (1024, 2 * T), 0)
    tail = lax.broadcasted_iota(jnp.int32, (T, 2 * T), 0) + 1024
    high = 1024 + lax.broadcasted_iota(jnp.int32, (1, 2 * T), 1) % T
    first_products(0)
    for b in range(4):
        here = slice(b * T, (b + 1) * T)
        span = slice(b * T, b * T + SPAN)
        if b == 1:
            x_second(0)
        if b < 3:
            first_products(b + 1)
        low = lo_ref[b:b + 1, :] - b * T
        low = jnp.concatenate([low, low], 1)
        scores = jnp.concatenate([
            jnp.where(spot >= low, sbuf[b % 2, 0:1024], NEG),
            jnp.where((tail >= low) & (tail <= high), sbuf[b % 2, 1024:SPAN], NEG)], 0)
        top = jnp.max(scores, axis=0, keepdims=True)
        expo = jnp.exp2((scores - top) * (SCALE * LOG2E))
        probs = expo * (1.0 / jnp.sum(expo, axis=0, keepdims=True))
        grad_probs = gbuf[b % 2]
        delta = jnp.sum(probs * grad_probs, axis=0, keepdims=True)
        grad_scores = (SCALE * probs * (grad_probs - delta)).astype(BF16)
        accv[span, :] += dims(probs.astype(BF16), pair(ob, b), 1, 0)
        acck[span, :] += dims(grad_scores, pair(qb, b), 1, 0)
        t2s[here, 0:T] = acck[here, :].astype(BF16)
        t2s[here, T:2 * T] = accv[here, :].astype(BF16)
        t2_copy(b).start()
        dq2 = dims(grad_scores, kv[span, 0:T], 0, 0).astype(BF16)
        dqs[here, 0:T] = dq2[:T]
        dqs[here, T:2 * T] = dq2[T:]

    owner = dev(jnp.where(core == 0, down, z), i, 1 - core)

    def t1_copy(part):
        return remote(t1s.at[part], tr1.at[part], t1_sem.at[0, part], t1_sem.at[1, part], owner)

    for part, total in enumerate((accv, acck)):
        t1s[part] = total[512:1024, :].astype(BF16)
        t1_copy(part).start()

    @pl.loop(1, 4)
    def _(b):
        x_second(b)

    @pl.loop(0, 4)
    def _(b):
        x_arrived(near_first(b))

    @pl.loop(0, 4)
    def _(b):
        t2_copy(b).wait_recv()

    right = lax.rem(y + 1, 4) * 2 + xh
    left = lax.rem(y + 3, 4) * 2 + xh

    def block(part, u, a, h):
        return gb.at[part, pl.ds(pl.multiple_of(a * HALF + h * 256, 256), 256), pl.ds(pl.multiple_of(u * T, T), T)]

    def d_copy(part, n, h):
        to = dev(z, (right, left, i)[n], own_half)
        return (gs.at[part, pl.ds(h * 256, 256)], block(part, y % 2, core, h), d_send.at[part, n, h],
                d_recv.at[part, (y % 2) * 4 + core * 2 + h], to)

    def forward(part, u, a, h):
        piece = block(part, u, a, h)
        n = u * 4 + a * 2 + h
        return remote(piece, piece, f_send.at[part, n], d_recv.at[part, n], dev(z, jnp.where(h == 0, right, left), core))

    def arrived(part, u, a, h):
        got(block(part, u, a, h), d_recv.at[part, u * 4 + a * 2 + h])

    def steps_from(u):
        return lax.rem(y - 2 * core - u + 8, 4)

    def first_send(part):
        for h in range(2):
            for n in range(2):
                src, dst, ssem, rsem, to = d_copy(part, n, (h + n) % 2)
                remote(src, dst, ssem, rsem, to).start()
        for h in range(2):
            src, dst, ssem, rsem, to = d_copy(part, 2, h)

            @pl.when(self_a)
            def _():
                pltpu.make_async_copy(src, dst, rsem).start()

            @pl.when(jnp.logical_not(self_a))
            def _():
                remote(src, dst, ssem, rsem, to).start()

    def forward_side(part):
        @pl.loop(0, 4)
        def _(e):
            u, a = e // 2, e % 2
            steps = steps_from(u)

            @pl.when((steps == 1) | (steps == 3))
            def _():
                h = jnp.where(steps == 1, 0, 1)
                arrived(part, u, a, h)
                forward(part, u, a, h).start()

    def gathered(part):
        @pl.loop(0, 4)
        def _(e):
            u, a = e // 2, e % 2
            steps = steps_from(u)

            @pl.when((steps == 2) | (steps == 0))
            def _():
                arrived(part, u, a, 0)
                arrived(part, u, a, 1)

            @pl.when((steps == 1) | (steps == 3))
            def _():
                arrived(part, u, a, jnp.where(steps == 1, 1, 0))

    def sent(part):
        for n in range(2):
            for h in range(2):
                src, dst, ssem, rsem, to = d_copy(part, n, h)
                remote(src, dst, ssem, rsem, to).wait_send()

        @pl.when(jnp.logical_not(self_a))
        def _():
            for h in range(2):
                src, dst, ssem, rsem, to = d_copy(part, 2, h)
                remote(src, dst, ssem, rsem, to).wait_send()

        @pl.loop(0, 4)
        def _(e):
            u, a = e // 2, e % 2
            steps = steps_from(u)

            @pl.when((steps == 1) | (steps == 3))
            def _():
                forward(part, u, a, jnp.where(steps == 1, 0, 1)).wait_send()

    def g_copy(part, m):
        col = pl.ds(pl.multiple_of(lane * T, T), T)
        return (gs.at[part, rows(0, m)], (dv_out, dk_out)[part].at[:, col], g_send.at[part, m], g_recv.at[part, lane],
                dev(z, 4 * core + m, own_half))

    def token_send(part):
        @pl.loop(0, 4)
        def _(m):
            mine = self_a & (m == lane)
            src, dst, ssem, rsem, to = g_copy(part, m)

            @pl.when(mine)
            def _():
                pltpu.make_async_copy(src, dst, rsem).start()

            @pl.when(jnp.logical_not(mine))
            def _():
                remote(src, dst, ssem, rsem, to).start()

    def token_wait(part):
        @pl.loop(0, 4)
        def _(m):
            got((dv_out, dk_out)[part].at[:, pl.ds(pl.multiple_of(m * T, T), T)], g_recv.at[part, m])
            src, dst, ssem, rsem, to = g_copy(part, m)

            @pl.when(jnp.logical_not(self_a & (m == lane)))
            def _():
                remote(src, dst, ssem, rsem, to).wait_send()

    for part, total in enumerate((accv, acck)):
        t1_copy(part).wait_recv()
        cols = pl.ds((1 - part) * T, T)
        gs[part] = (total[1024:1536, :] + tr1[part].astype(F32) + tr2[:, cols].astype(F32)).astype(BF16)
        first_send(part)


    def dest(offset):
        return lax.rem(z + offset + NZ, NZ)

    def long_copy(part, sub, h, k):
        slot, ii = (xh, (i // 2) * 2 + sub) if k == 3 else (sub, i)
        return remote(sdn.at[part, sub, h, k], rdn.at[part, slot, h, k], dn_send.at[part, sub, h, k],
                      dn_recv.at[part, slot, h, k], dev(down if sub == 0 else up, ii, core))

    def short_copy(part, sub, h, k):
        slot, ii = (xh, (i // 2) * 2 + sub) if k == 2 else (sub, i)
        return remote(sup.at[part, sub, h, k], rup.at[part, slot, h, k], up_send.at[part, sub, h, k],
                      up_recv.at[part, slot, h, k], dev(up if sub == 0 else down, ii, core))

    def ring(part, k):
        for h in range(2):
            lines = slice(h * 48, h * 48 + 48)
            for sub in range(2):
                way = -1 if sub == 0 else 1
                value = pbuf[part, sub, dest(way * (4 - k)), lines]
                if k > 0:
                    got(rdn.at[part, sub, h, k - 1], dn_recv.at[part, sub, h, k - 1])
                    value = value + rdn[part, sub, h, k - 1].astype(F32)
                sdn[part, sub, h, k] = value.astype(BF16)
                long_copy(part, sub, h, k).start()
            if k < 3:
                for sub in range(2):
                    way = -1 if sub == 0 else 1
                    value = pbuf[part, sub, dest(-way * (3 - k)), lines]
                    if k > 0:
                        got(rup.at[part, sub, h, k - 1], up_recv.at[part, sub, h, k - 1])
                        value = value + rup[part, sub, h, k - 1].astype(F32)
                    sup[part, sub, h, k] = value.astype(BF16)
                    short_copy(part, sub, h, k).start()

    def product(part):
        @pl.loop(0, 4)
        def _(n):
            at = pl.ds((n % 2) * 4, 4)
            lhs = jnp.concatenate([xb[n // 2, j, at].reshape(384, T) for j in range(8)], 1)
            pbuf[part, n // 2, at] = jnp.dot(lhs, gb[part], preferred_element_type=F32).reshape(4, 96, 256)

    def p_copy(part):
        return remote(pbuf.at[part, 1 - xh, z], precv.at[part], p_sem.at[0, part], p_sem.at[1, part], dev(z, flip, core))

    offset = 4 * (i % 4)

    def weight_copy(part):
        return pltpu.make_async_copy(fin.at[part], (wv_out, wk_out)[part], out_sem.at[part])

    def finish(part):
        p_copy(part).wait_recv()
        for s in range(2):
            pieces = []
            for h in range(2):
                got(rdn.at[part, s, h, 3], dn_recv.at[part, s, h, 3])
                got(rup.at[part, s, h, 2], up_recv.at[part, s, h, 2])
                pieces.append(rdn[part, s, h, 3].astype(F32) + rup[part, s, h, 2].astype(F32))
            total = jnp.concatenate(pieces, 0) + jnp.where(xh == s, pbuf[part, s, z], precv[part])
            total = pltpu.roll(total, lax.rem(96 - offset, 96), 0)
            for u in range(2):
                fin[part, :, (u * 2 + s) * T:(u * 2 + s + 1) * T] = total[:84, u * T:(u + 1) * T]
        weight_copy(part).start()

    forward_side(0)
    forward_side(1)

    @pl.loop(0, 4)
    def _(b):
        x_third(b)

    gathered(0)
    x_complete()
    product(0)
    ring(0, 0)
    p_copy(0).start()
    @pl.loop(0, 4)
    def _(b):
        mine = self_a & (b == lane)
        src, dst, ssem, rsem, to = dq_copy(b)

        @pl.when(mine)
        def _():
            pltpu.make_async_copy(src, dst, rsem).start()

        @pl.when(jnp.logical_not(mine))
        def _():
            remote(src, dst, ssem, rsem, to).start()

    token_send(0)
    token_send(1)
    gathered(1)
    product(1)
    ring(1, 0)
    p_copy(1).start()
    ring(0, 1)
    ring(1, 1)
    ring(0, 2)
    ring(1, 2)
    ring(0, 3)
    ring(1, 3)
    finish(0)
    finish(1)
    token_wait(0)
    token_wait(1)

    @pl.loop(0, 4)
    def _(l):
        got(dq_out.at[:, pl.ds(pl.multiple_of(l * 2 * T, 2 * T), 2 * T)], dq_recv.at[l])

    @pl.loop(0, 4)
    def _(m):
        z_copy(m).wait_send()
        s_copy(m).wait_send()
        src, dst, ssem, rsem, to = dq_copy(m)

        @pl.when(jnp.logical_not(self_a & (m == lane)))
        def _():
            for src_a, dst_a, ssem_a, rsem_a in a_parts(m):
                remote(src_a, dst_a, ssem_a, rsem_a, dev(z, 4 * core + m, own_half)).wait_send()
            remote(src, dst, ssem, rsem, to).wait_send()

    @pl.loop(0, 4)
    def _(b):
        t2_copy(b).wait_send()


    @pl.loop(0, 4)
    def _(ys):
        x_across(ys).wait_send()
        x_beside(ys).wait_send()
        xs_own(ys).wait_send()
        for s in range(2):
            xs_other(ys, s).wait_send()

    @pl.loop(1, 4)
    def _(step):
        for sub in range(2):
            x_copy(step, sub).wait_send()

    for part in range(2):
        t1_copy(part).wait_send()
        sent(part)
        weight_copy(part).wait()
        p_copy(part).wait_send()
        for sub in range(2):
            for h in range(2):
                for k in range(4):
                    long_copy(part, sub, h, k).wait_send()
                for k in range(3):
                    short_copy(part, sub, h, k).wait_send()


def copies(*refs):
    count = 5
    inputs, outputs, held, sem = refs[:count], refs[count:2 * count], refs[2 * count:3 * count], refs[-1]
    loads = [pltpu.make_async_copy(inputs[n], held[n], sem.at[0, n]) for n in range(count)]
    stores = [pltpu.make_async_copy(held[n], outputs[n], sem.at[1, n]) for n in range(count)]
    for load in loads:
        load.start()
    for load, store in zip(loads, stores):
        load.wait()
        store.start()
    for store in stores:
        store.wait()


def local(inputs, queries, keys, values, grad_out, doc_ids):
    x = inputs.reshape(8, 672, 128)
    docs = doc_ids.reshape(64, 128)
    anywhere = pl.BlockSpec(memory_space=pl.ANY)
    dma = pltpu.SemaphoreType.DMA
    shape = jax.ShapeDtypeStruct
    vmem = pltpu.VMEM
    outs = (
        shape((T, 1024), BF16), shape((T, 512), BF16), shape((T, 512), BF16), shape((84, 512), F32), shape((84, 512), F32))
    results = pl.pallas_call(
        kernel,
        name="window_backward",
        out_shape=outs,
        in_specs=[anywhere] * 6,
        out_specs=(anywhere,) * 5,
        scratch_shapes=[
            vmem((512, 256), BF16), vmem((512, 256), BF16), vmem((WIN, 256), BF16),
            vmem((2, 8, 8, 96, T), BF16), vmem((WIN, T), F32), vmem((WIN, T), F32),
            vmem((8, T), jnp.int32), vmem((512, 256), BF16),
            vmem((2, 512, T), BF16), vmem((2, 512, T), BF16), vmem((512, 256), BF16), vmem((512, 256), BF16),
            vmem((2, 512, T), BF16), vmem((2, 1024, 256), BF16),
            vmem((2, 2, 8, 96, 256), F32),
            vmem((2, 2, 2, 4, 48, 256), BF16), vmem((2, 2, 2, 3, 48, 256), BF16),
            vmem((2, 2, 2, 4, 48, 256), BF16), vmem((2, 2, 2, 3, 48, 256), BF16), vmem((64, 128), jnp.int32), vmem((2, 84, 512), F32),
            vmem((2, 96, 256), F32), vmem((2, SPAN, 256), F32), vmem((2, SPAN, 256), F32),
            dma((4, 4)), dma((4, 2)), dma((4, 2)), dma((4,)), dma((4,)), dma((4,)), dma((4,)), dma((4, 2)), dma((4, 2)), dma((4, 3)), dma((4, 3)),
            dma((4,)), dma((4,)), dma((2, 2)), dma((2, 4)), dma((2, 3, 2)), dma((2, 8)), dma((2, 8)),
            dma((2, 2, 2, 4)), dma((2, 2, 2, 4)), dma((2, 2, 2, 3)), dma((2, 2, 2, 3)), dma(()), dma((2,)), dma((2, 4)), dma((2, 4)),
            dma((2, 2)), dma((4,)), dma((4,)), dma((4,)), dma((4,)),
        ],
        compiler_params=pltpu.CompilerParams(
            collective_id=0, has_side_effects=True, vmem_limit_bytes=60 << 20),
        cost_estimate=pl.CostEstimate(flops=3_000_000_000, bytes_accessed=12_000_000, transcendentals=1_200_000),
    )(x, queries, keys, values, grad_out, docs)
    return tuple(pl.pallas_call(
        copies,
        name="results",
        out_shape=outs,
        in_specs=[anywhere] * 5,
        out_specs=(anywhere,) * 5,
        scratch_shapes=[vmem(o.shape, o.dtype) for o in outs] + [dma((2, 5))],
        compiler_params=pltpu.CompilerParams(vmem_limit_bytes=60 << 20),
    )(*results))


def solution(mesh):
    return jax.shard_map(
        local,
        mesh=mesh,
        in_specs=(P(None, "seq"), P("seq", "head"), P("seq", "head"), P("seq", "head"), P("seq", "head"), P()),
        out_specs=(P("seq", "head"),) * 5,
        check_vma=False,
    )
```
